128 devices in a mesh: role: 2 (over z_hi), dev: 64 (over z_lo, y, x, core).
Axes of the slice: x: 4, y: 4, z: 4 (z_hi: 2, z_lo: 2; z = z_hi * 2 + z_lo), core: 2. Of those that a mesh axis runs over, the one named last changes fastest.
Arguments:
- queries: bfloat16 [512, 64, 576], P(('role', 'dev')), may hold values from -14 to 14
- latent_cache: bfloat16 [512, 512, 576], P(('role', 'dev')), may hold values from -4 to 4
- cache_lengths: int32 [512], P(('role', 'dev')), may hold values from 1 to 512, 163840 in all
- residual: bfloat16 [512, 7168], P(('role', 'dev')), may hold values from -26 to 26
- expert_ids: int32 [512, 8], P(('role', 'dev')), may hold values from 0 to 15, all different within a row; in each aligned block of 2 rows (0 to 1, 2 to 3, ...) at most 2 rows name the same one
- route_weights: float32 [512, 8], P(('role', 'dev')), may hold values from 0.05 to 0.5
- value_weight: bfloat16 [64, 512, 128], P('dev'), may hold values from -2.5 to 2.5
- w_out: bfloat16 [8192, 7168], P('dev'), may hold values from -0.0625 to 0.0625
- w_gate: bfloat16 [128, 7168, 256], P(('role', 'dev')), may hold values from -0.0625 to 0.0625
- w_up: bfloat16 [128, 7168, 256], P(('role', 'dev')), may hold values from -0.0625 to 0.0625
- w_down: bfloat16 [128, 256, 7168], P(('role', 'dev')), may hold values from -0.125 to 0.125
Outputs:
- layer_out: bfloat16 [512, 7168], P(('role', 'dev'))
The draws below stay inside these ranges and needn't reach their ends.
Inputs may be any that keep to these rules, and one draw needn't show every extreme that they name: `expert_ids`: in every aligned block of 2 rows no expert is named by more than 2 rows.
All inputs are finite; a program needn't handle non-finite values. No bound on the sum of `cache_lengths` on one device may be relied on, other than what follows from the above.
Results may differ from the reference program's by a relative error of at most 0.006.
Values may be sent and summed in bfloat16 or wider, within the bound.
A program may use at most 128 MiB of HBM per device.

```python
import math
import jax
import jax.numpy as jnp
import numpy as np
from jax import lax

D = 7168
FF = 2048
LOCAL_HEADS = 64
KEY_VALUE_RANK = 512
VALUE_HEAD_WIDTH = 128
TOP = 8
EXPERTS = 16
MB_ROWS = 2
LEN = 512
LATENT = 576
ROW_DEV = 4
REQUEST_COUNT = 512
SPLIT = 8
FF_DEV = 256
CAP = 2
DEVICES = 128


def draw_latent_cache(key, part):
    key = jax.random.fold_in(key, 11)
    field = jnp.clip(jax.random.normal(key, (REQUEST_COUNT, LEN, LATENT), jnp.float32), -4.0, 4.0)
    return field.astype(jnp.bfloat16)


def draw_queries(key, part):
    key = jax.random.fold_in(key, 12)
    field = jnp.clip(jax.random.normal(key, (REQUEST_COUNT, LOCAL_HEADS, LATENT), jnp.float32), -4.0, 4.0)
    return field.astype(jnp.bfloat16)


def draw_residual(key, part):
    key = jax.random.fold_in(key, 13)
    first, second, third = jax.random.split(key, 3)
    column_scale = jnp.exp(jax.random.uniform(first, (1, D), jnp.float32, math.log(0.5), math.log(2.5)))
    row_scale = jnp.exp(jax.random.uniform(second, (REQUEST_COUNT, 1), jnp.float32, math.log(0.5), math.log(2.5)))
    field = jnp.clip(jax.random.normal(third, (REQUEST_COUNT, D), jnp.float32), -4.0, 4.0)
    return (field * column_scale * row_scale).astype(jnp.bfloat16)


def block_scale(rng, shape, shards, least, largest):
    def one(axis_at, blocks):
        steps = jax.random.uniform(jax.random.fold_in(jax.random.fold_in(rng, 6), axis_at), (blocks,), jnp.float32, least / len(shards), largest / len(shards))
        return jnp.repeat(jnp.exp(steps), shape[axis_at] // blocks).reshape((-1,) + (1,) * (len(shape) - axis_at - 1))

    level = one(*shards[0])
    for cut in shards[1:]:
        level = level * one(*cut)
    return level


def split_up(count, total, most, slope):
    loads = [(1 << 20) // math.isqrt(rank ** slope) + 1 for rank in range(2, count + 1)]
    spare, counts = total - most - (count - 1), [1] * (count - 1)
    while spare > 0:
        free = [i for i in range(count - 1) if counts[i] < most]
        whole, budget = sum([loads[i] for i in free]), spare
        for i in free:
            addition = min(most - counts[i], max(1, budget * loads[i] // whole), spare)
            counts[i] = counts[i] + addition
            spare = spare - addition
    return np.array([most] + counts)


def uneven(own_key, count, total, reach, slope):
    if count == 2:
        one = jax.random.randint(own_key, (), max(1, total - reach), min(reach, total - 1) + 1)
        return jnp.stack([one, total - one])
    sizes = jnp.asarray(split_up(count, total, reach, slope), jnp.int32)
    pairs = (count - 1) // 2
    donor, taker = sizes[1:1 + 2 * pairs:2], sizes[2:2 + 2 * pairs:2]
    slack = jnp.minimum(donor - 1, reach - taker)
    shifted = jax.random.randint(jax.random.fold_in(own_key, 1), (pairs,), 0, 1 << 20) % (slack + 1)
    sizes = sizes.at[1:1 + 2 * pairs:2].set(donor - shifted).at[2:2 + 2 * pairs:2].set(taker + shifted)
    return sizes[jax.random.permutation(jax.random.fold_in(own_key, 2), count)]


def deal_out(rng, own, number, rows, count, top, most, slope):
    sequence = jax.random.permutation(rng, count)
    crowded, usual = shares(count, rows * top, most, slope, True), shares(count, rows * top, most, slope, False)
    places = jnp.arange(count)

    def named(tallies, turn):
        used = int((tallies > 0).sum())
        fixed = max(1, used // 4)
        moved = fixed + (places - fixed + turn * (used - fixed)) % max(1, count - fixed)
        return jnp.zeros((count,), jnp.int32).at[sequence[jnp.where(places < fixed, places, moved)]].set(jnp.asarray(tallies, jnp.int32))

    tallies = jnp.where(number % 4 == 0, named(crowded, number // 4), named(usual, number - number // 4 - 1))
    mixed = jax.random.permutation(jax.random.fold_in(own, 3), count)
    source_of, taker = mixed[0:count // 2 * 2:2], mixed[1:count // 2 * 2:2]
    room = jnp.minimum(tallies[source_of] - 1, most - tallies[taker]) // 2
    room = jnp.where((source_of == sequence[0]) | (taker == sequence[0]) | (tallies[taker] == 0), 0, jnp.maximum(room, 0))
    moved = jax.random.randint(jax.random.fold_in(own, 4), (count // 2,), 0, 1 << 20) % (room + 1)
    tallies = tallies.at[source_of].add(-moved).at[taker].add(moved)
    items = jnp.searchsorted(jnp.cumsum(tallies), jnp.arange(rows * top), side="right").astype(jnp.int32)
    table = items.reshape(top, rows).T
    table = table[jax.random.permutation(jax.random.fold_in(own, 1), rows)]
    turn = jax.random.randint(jax.random.fold_in(own, 2), (rows, 1), 0, top)
    return jnp.take_along_axis(table, (jnp.arange(top)[None, :] + turn) % top, axis=1)


def shares(count, total, limit, lean, full):
    portions = [(1 << 20) // math.isqrt(rank ** lean) + 1 for rank in range(1, count + 1)]
    largest = limit if full else min(limit, max(-(-total // count), total * portions[0] // sum(portions)))
    least = 1 if total - largest >= count - 1 else 0
    holding, spare = [largest] + [least] * (count - 1), total - largest - least * (count - 1)
    while spare > 0:
        movable = [i for i in range(1, count) if holding[i] < largest] or [i for i in range(1, count) if holding[i] < limit]
        whole, budget = sum([portions[i] for i in movable]), spare
        for i in movable:
            extra = min(limit - holding[i], max(1, budget * portions[i] // whole), spare)
            holding[i] = holding[i] + extra
            spare = spare - extra
    return np.array(holding)


def scatter_about(own_key, dims, scale, limit, cuts=(), kind=jnp.bfloat16):
    gain = block_scale(own_key, dims, cuts, -0.22, 0.18) if cuts else 1.0
    entries = jax.random.normal(own_key, dims, jnp.float32) * scale * gain
    return jnp.minimum(jnp.maximum(entries, -limit), limit).astype(kind)


def setup_inputs(seed: int = 0) -> dict:
    splits = jax.random.split(jax.random.key(seed), 12)
    queries = draw_queries(jax.random.fold_in(splits[11], 71), 0)
    latent_cache = draw_latent_cache(jax.random.fold_in(splits[11], 71), 0)
    cache_lengths = uneven(splits[2], REQUEST_COUNT, REQUEST_COUNT * LEN * 5 // 8, LEN, 1).astype(jnp.int32)
    residual = draw_residual(jax.random.fold_in(splits[11], 71), 0)
    expert_ids_keys = jax.random.split(jax.random.fold_in(splits[4], 1), REQUEST_COUNT // MB_ROWS)
    expert_ids_turns = jax.random.permutation(jax.random.fold_in(splits[4], 3), REQUEST_COUNT // MB_ROWS)
    expert_ids = jax.vmap(lambda own, number: deal_out(jax.random.fold_in(splits[4], 2), own, number, MB_ROWS, EXPERTS, TOP, CAP, 1))(expert_ids_keys, expert_ids_turns).reshape((REQUEST_COUNT, TOP))
    route_weights = jnp.clip(jnp.exp(math.log(0.5) - 2.3025851 * jax.random.uniform(splits[5], (REQUEST_COUNT, TOP), jnp.float32) ** block_scale(splits[5], (REQUEST_COUNT, TOP), ((0, 128),), -0.2, 0.2)), 0.05, 0.5)
    value_weight = scatter_about(splits[6], (LOCAL_HEADS, KEY_VALUE_RANK, VALUE_HEAD_WIDTH), (4 * KEY_VALUE_RANK ** -0.5), 2.5, ((0, 64),))
    w_out = scatter_about(splits[7], (LOCAL_HEADS * VALUE_HEAD_WIDTH, D), (LOCAL_HEADS * VALUE_HEAD_WIDTH) ** -0.5, 0.0625, ((0, 64),))
    w_gate = scatter_about(splits[8], (DEVICES, D, FF_DEV), D ** -0.5, 0.0625, ((0, 128),))
    w_up = scatter_about(splits[9], (DEVICES, D, FF_DEV), D ** -0.5, 0.0625, ((0, 128),))
    w_down = scatter_about(splits[10], (DEVICES, FF_DEV, D), FF ** -0.5, 0.125, ((0, 128),))
    return {"queries": queries, "latent_cache": latent_cache, "cache_lengths": cache_lengths, "residual": residual, "expert_ids": expert_ids, "route_weights": route_weights, "value_weight": value_weight, "w_out": w_out, "w_gate": w_gate, "w_up": w_up, "w_down": w_down}


score_scale = 1.0 / math.sqrt(192.0)

def attend(query, latent_store, length):
    scores = jnp.einsum('nhl,ntl->nht', query.astype(jnp.float32), latent_store.astype(jnp.float32)) * score_scale
    living = jnp.arange(latent_store.shape[1], dtype=jnp.int32)[None, None, :] < length[:, None, None]
    scores = jnp.where(living, scores, -jnp.inf)
    highest = lax.optimization_barrier(jnp.max(scores, -1, keepdims=True))
    raised = jnp.exp(scores - highest)
    chances = (raised / lax.optimization_barrier(jnp.sum(raised, -1, keepdims=True))).astype(jnp.bfloat16)
    latent_content = latent_store[:, :, :KEY_VALUE_RANK].astype(jnp.float32)
    return jnp.einsum('nht,ntk->nhk', chances.astype(jnp.float32), latent_content).astype(jnp.bfloat16)

def rms_normed(hidden):
    widened = hidden.astype(jnp.float32)
    return (widened * lax.rsqrt(lax.optimization_barrier(jnp.mean(widened * widened, -1, keepdims=True)) + 1e-06)).astype(jnp.bfloat16)

def routing(expert_ids, route_weights):
    row_count = expert_ids.shape[0]
    onehot = (expert_ids[:, :, None] == jnp.arange(EXPERTS, dtype=jnp.int32)[None, None, :]).astype(jnp.float32)
    row_hits = lax.optimization_barrier(jnp.sum(onehot, 1))
    earlier = (jnp.arange(row_count, dtype=jnp.int32)[:, None] > jnp.arange(row_count, dtype=jnp.int32)[None, :]).astype(jnp.float32)
    counted = jnp.dot(earlier, row_hits, precision=lax.Precision.HIGHEST)
    slot_index = lax.optimization_barrier(jnp.sum(onehot * counted[:, None, :], -1))
    slot_onehot = (slot_index[:, :, None] == jnp.arange(CAP, dtype=jnp.float32)[None, None, :]).astype(jnp.float32)
    placing = jnp.einsum('rke,rkc->rec', onehot, slot_onehot, precision=lax.Precision.HIGHEST)
    weighting = jnp.einsum('rke,rkc->rec', onehot * route_weights[:, :, None], slot_onehot, precision=lax.Precision.HIGHEST)
    return (placing, weighting)

def reference(queries, latent_cache, cache_lengths, residual, expert_ids, route_weights, value_weight, w_out, w_gate, w_up, w_down):

    def attend_block(packed):
        return attend(packed[0], packed[1], packed[2])
    latent_result = lax.map(attend_block, (queries.reshape(DEVICES, ROW_DEV, LOCAL_HEADS, LATENT), latent_cache.reshape(DEVICES, ROW_DEV, LEN, LATENT), cache_lengths.reshape(DEVICES, ROW_DEV)))
    latent_result = latent_result.reshape(REQUEST_COUNT, LOCAL_HEADS, KEY_VALUE_RANK)
    value_per_head = jnp.einsum('ztw,twr->ztr', latent_result.astype(jnp.float32), value_weight.astype(jnp.float32)).astype(jnp.bfloat16)
    attended = jnp.dot(value_per_head.reshape(REQUEST_COUNT, LOCAL_HEADS * VALUE_HEAD_WIDTH), w_out, preferred_element_type=jnp.float32)
    hidden = (residual.astype(jnp.float32) + attended).astype(jnp.bfloat16)
    normed = rms_normed(hidden)
    blocks = REQUEST_COUNT // MB_ROWS
    placing, weighting = jax.vmap(routing)(expert_ids.reshape(blocks, MB_ROWS, TOP), route_weights.reshape(blocks, MB_ROWS, TOP))
    buffers = jnp.einsum('brec,brd->ebcd', placing, normed.reshape(blocks, MB_ROWS, D).astype(jnp.float32), precision=lax.Precision.HIGHEST).astype(jnp.bfloat16)

    def expert_block(packed):
        row_block, gate_part, up_part, down_part = packed
        gate_full = jnp.transpose(gate_part, (1, 0, 2)).reshape(D, FF)
        up_full = jnp.transpose(up_part, (1, 0, 2)).reshape(D, FF)
        gate_act = jnp.dot(row_block, gate_full, preferred_element_type=jnp.float32)
        up_act = jnp.dot(row_block, up_full, preferred_element_type=jnp.float32)
        activated = (jax.nn.silu(gate_act) * up_act).astype(jnp.bfloat16)
        pieces = activated.reshape(row_block.shape[0], SPLIT, FF_DEV).astype(jnp.float32)
        partial_out = jnp.einsum('nsf,sfd->snd', pieces, down_part.astype(jnp.float32)).astype(jnp.bfloat16)
        return lax.optimization_barrier(jnp.sum(partial_out.astype(jnp.float32), 0))
    expert_outputs = lax.map(expert_block, (buffers.reshape(EXPERTS, blocks * CAP, D), w_gate.reshape(EXPERTS, SPLIT, D, FF_DEV), w_up.reshape(EXPERTS, SPLIT, D, FF_DEV), w_down.reshape(EXPERTS, SPLIT, FF_DEV, D)))
    expert_outputs = expert_outputs.reshape(EXPERTS, blocks, CAP, D)
    mixture = jnp.einsum('brec,ebcd->brd', weighting, expert_outputs, precision=lax.Precision.HIGHEST).reshape(REQUEST_COUNT, D)
    return (hidden.astype(jnp.float32) + mixture).astype(jnp.bfloat16)
```

```python
import math

import jax
import jax.numpy as jnp
from jax import lax
from jax.experimental import pallas as pl
from jax.experimental.pallas import tpu as pltpu
from jax.sharding import PartitionSpec as P

KEY_VALUE_RANK = 512
EXPERTS = 16
MESH = pl.DeviceIdType.MESH
D = 7168
Q = D // 4
FF = 256
HEAD = 128
BF = jnp.bfloat16
F32 = jnp.float32
score_scale = 1.0 / math.sqrt(192.0)


def attend(query, latent_store, length):
    scores = (
        jnp.einsum("nhl,ntl->nht", query, latent_store, preferred_element_type=jnp.float32)
        * score_scale
    )
    living = (
        jnp.arange(latent_store.shape[1], dtype=jnp.int32)[None, None, :] < length[:, None, None]
    )
    scores = jnp.where(living, scores, -jnp.inf)
    highest = jnp.max(scores, -1, keepdims=True)
    raised = jnp.exp(scores - highest)
    chances = (raised / jnp.sum(raised, -1, keepdims=True)).astype(jnp.bfloat16)
    latent_content = latent_store[:, :, :KEY_VALUE_RANK]
    return jnp.einsum(
        "nht,ntk->nhk", chances, latent_content, preferred_element_type=jnp.float32
    ).astype(jnp.bfloat16)


def parts_of(tiles):
    offset, parts = 0, []
    for count in tiles:
        parts.append((offset * 128, count * 128))
        offset += count
    assert offset * 128 == Q
    return parts


B_PARTS = parts_of((3, 3, 3, 3, 2))
B_BITS = ("x1", "y1", "z0", "x0", "y0")
C_PARTS = parts_of((3, 2, 2, 3, 2, 2))
C_BITS = ("x1", "y1", "z1", "x0", "y0", "z0")
B_DIMS = ("z0", "y1", "y0", "x1", "x0")
C_DIMS = ("z1",) + B_DIMS
T_DIMS = ("z1", "z0", "y1", "y0")
EVERY = slice(None)


class Sems:
    def __init__(self, sends, recvs):
        self.sends, self.recvs, self.count, self.pending = sends, recvs, 0, []

    def remote(self, source, target, landing, device):
        n = self.count
        self.count += 1
        copy = pltpu.make_async_remote_copy(
            src_ref=source,
            dst_ref=target,
            send_sem=self.sends.at[n],
            recv_sem=self.recvs.at[n],
            device_id=device,
            device_id_type=MESH,
        )
        copy.start()
        self.pending.append(copy)
        return pltpu.make_async_remote_copy(
            src_ref=source,
            dst_ref=landing,
            send_sem=self.sends.at[n],
            recv_sem=self.recvs.at[n],
            device_id=device,
            device_id_type=MESH,
        ).wait_recv


SEMS = 136


def kernel(
    rel_ref, res_ref, wts_ref, vw_ref, wo_hbm, wg_hbm, wu_hbm, wd_hbm, out_ref,
    wo, wg, wu, wd, resx, wx, hid, sb, ab, rbc, rb, ss, ssr, tab, g, accg, accu, act,
    sh, ah, rhc, rh, outs, fsend, frecv, loads, sends, recvs,
):
    role, dev = lax.axis_index("role"), lax.axis_index("dev")
    core, x, y, zl = dev % 2, (dev // 2) % 4, (dev // 8) % 4, dev // 32
    own = {
        "x1": x // 2, "x0": (x + x // 2) % 2, "y1": y // 2, "y0": (y + y // 2) % 2,
        "z1": role, "z0": (zl + role) % 2,
    }
    partner = {
        "core": (role, dev + 1 - 2 * core),
        "x1": (role, dev + 2 * (3 - 2 * x)),
        "x0": (role, dev + 2 * (1 - 2 * (x % 2))),
        "xd": (role, dev + 2 * ((x + 2) % 4 - x)),
        "y1": (role, dev + 8 * (3 - 2 * y)),
        "y0": (role, dev + 8 * (1 - 2 * (y % 2))),
        "z1": (1 - role, dev + 32 * (1 - 2 * zl)),
        "z0": (role, dev + 32 * (1 - 2 * zl)),
    }
    sibling = 1 - core

    fetch = []

    def load(source, target):
        copy = pltpu.make_async_copy(source, target, loads.at[len(fetch)])
        copy.start()
        fetch.append(copy)
        return copy

    wo_loads = [load(wo_hbm.at[:, pl.ds(q * Q, Q)], wo.at[q]) for q in range(4)]
    wg_load, wu_load = load(wg_hbm, wg), load(wu_hbm, wu)
    wd_loads = [load(wd_hbm.at[:, pl.ds(q * Q, Q)], wd.at[q]) for q in range(4)]

    barrier = pltpu.get_barrier_semaphore()
    for device in partner.values():
        pl.semaphore_signal(barrier, inc=1, device_id=device, device_id_type=MESH)
    pl.semaphore_wait(barrier, len(partner))

    sems = Sems(sends, recvs)
    x1, x0 = own["x1"], own["x0"]
    lines = (("x0", x1, 1 - x0), ("x1", 1 - x1, x0), ("xd", 1 - x1, 1 - x0))

    arrivals = []
    for name, p1, p0 in lines:
        arrivals.append(sems.remote(res_ref.at[p1, p0], resx.at[x1, x0], resx.at[p1, p0], partner[name]))
        arrivals.append(sems.remote(wts_ref, wx.at[x1, x0], wx.at[p1, p0], partner[name]))
    resx[x1, x0] = res_ref[x1, x0]
    wx[x1, x0] = wts_ref[...]

    for copy in wo_loads:
        copy.wait()

    def project(half, target):
        values = jnp.dot(rel_ref[half], vw_ref[...], preferred_element_type=F32).astype(BF)

        def quarter(q):
            product = jnp.dot(values, wo[q], preferred_element_type=F32).astype(BF)
            target[:, :, :, q // 2, q % 2] = product.reshape(2, 2, 2, 16, Q)

        return quarter

    quarter = project(sibling, sb)
    waits = []
    for q in range(4):
        quarter(q)
        where = (EVERY, EVERY, EVERY, q // 2, q % 2)
        waits.append(sems.remote(sb.at[where], rbc.at[where], rbc.at[where], partner["core"]))
    quarter = project(core, ab)
    for q in range(4):
        quarter(q)
    for q in range(4):
        waits[q]()
        where = (EVERY, EVERY, EVERY, q // 2, q % 2)
        ab[where] = ab[where] + rbc[where]

    def reduce_scatter(buf, landing, dims, bits, parts):
        number = len(bits)
        waits = {}

        def place(k, step, current):
            order = [bits[(k + j) % number] for j in range(number)]
            indices = []
            for dim in dims:
                at = order.index(dim)
                if at < step:
                    indices.append(own[dim])
                elif at == step:
                    indices.append(own[dim] if current else 1 - own[dim])
                else:
                    indices.append(EVERY)
            return tuple(indices) + (EVERY, pl.ds(*parts[k])), order[step]

        for step in range(number):
            for k in range(len(parts)):
                if step:
                    waits[k]()
                    mine, _ = place(k, step - 1, True)
                    other, _ = place(k, step - 1, False)
                    buf[mine] = buf[mine] + landing[other]
                mine, bit = place(k, step, True)
                other, _ = place(k, step, False)
                waits[k] = sems.remote(buf.at[other], landing.at[mine], landing.at[other], partner[bit])
        last = []
        for k in range(len(parts)):
            waits[k]()
            mine, _ = place(k, number - 1, True)
            other, _ = place(k, number - 1, False)
            last.append((parts[k], mine, other))
        return last

    last = reduce_scatter(ab, rb, B_DIMS, B_BITS, B_PARTS)

    for wait in arrivals:
        wait()
    for j in range(4):
        hid[4 * j:4 * j + 4, :] = resx[j // 2, j % 2]
    block = tuple(own[dim] for dim in C_DIMS)
    squares = jnp.zeros((16, 1), F32)
    for (start, width), mine, other in last:
        columns = pl.ds(start, width)
        total = hid[:, columns] + (ab[mine].astype(F32) + rb[other].astype(F32))
        rounded = total.astype(BF)
        g[(core,) + block + (EVERY, columns)] = rounded
        total = rounded.astype(F32)
        hid[:, columns] = total
        squares = squares + jnp.sum(total * total, axis=1, keepdims=True)
    ss[0] = jnp.broadcast_to(squares, (16, 128))

    def gather_place(k, step, mine, bits, dims):
        number = len(bits)
        order = [bits[(k + number - 1 - j) % number] for j in range(number)]
        indices = []
        for dim in dims:
            at = order.index(dim)
            if at < step:
                indices.append(EVERY)
            elif at == step:
                indices.append(own[dim] if mine else 1 - own[dim])
            else:
                indices.append(own[dim])
        return tuple(indices), order[step]

    waits, forwards = {}, []
    table_waits = []
    t_bits = ("y0", "y1", "z0", "z1")
    lanes = lax.broadcasted_iota(jnp.int32, (16, 128), 1)
    steps = len(C_BITS)
    for step in range(steps + 1):
        for k in range(len(C_PARTS)):
            tail = (EVERY, pl.ds(*C_PARTS[k]))
            if step:
                waits[k]()
            if step < steps:
                mine, bit = gather_place(k, step, True, C_BITS, C_DIMS)
                other, _ = gather_place(k, step, False, C_BITS, C_DIMS)
                here = g.at[(core,) + mine + tail]
                waits[k] = sems.remote(here, here, g.at[(core,) + other + tail], partner[bit])
            if step >= steps - 1:
                mine, _ = gather_place(k, steps - 1, step == steps - 1, C_BITS, C_DIMS)
                here = g.at[(core,) + mine + tail]
                forwards.append(sems.remote(here, here, g.at[(sibling,) + mine + tail], partner["core"]))
        if step < 2:
            table_waits.append(sems.remote(ss.at[step], ssr.at[step], ssr.at[step], partner[("x0", "x1")[step]]))
            table_waits[-1]()
            ss[step + 1] = ss[step] + ssr[step]
            if step == 1:
                weights = jnp.concatenate([wx[j // 2, j % 2] for j in range(4)], axis=0)
                scale = lax.rsqrt(ss[2] * (1.0 / D) + 1e-06)
                tab[(core,) + tuple(own[dim] for dim in T_DIMS)] = jnp.where(lanes == EXPERTS, scale, weights)
        elif step < 6:
            if step > 2:
                table_waits[-1]()
            mine, bit = gather_place(3, step - 2, True, t_bits, T_DIMS)
            other, _ = gather_place(3, step - 2, False, t_bits, T_DIMS)
            here = tab.at[(core,) + mine]
            table_waits.append(sems.remote(here, here, tab.at[(core,) + other], partner[bit]))
        else:
            table_waits[-1]()
            table_waits.append(sems.remote(tab.at[core], tab.at[core], tab.at[sibling], partner["core"]))

    wg_load.wait()
    wu_load.wait()
    expert = role * 8 + zl * 4 + y
    rows_lanes = lax.broadcasted_iota(jnp.int32, (256, 128), 1)

    def gate_up(half):
        accg[...] = jnp.zeros_like(accg)
        accu[...] = jnp.zeros_like(accu)

        def quarter(q, carry):
            rows = g[half, :, :, :, :, q // 2, q % 2].reshape(256, Q)
            accg[...] += jnp.dot(rows, wg[q], preferred_element_type=F32)
            accu[...] += jnp.dot(rows, wu[q], preferred_element_type=F32)
            return carry

        lax.fori_loop(0, 4, quarter, 0)

    def activate(half):
        table = tab[half].reshape(256, 128)
        weight = jnp.sum(jnp.where(rows_lanes == expert, table, 0.0), axis=1, keepdims=True)
        scale = jnp.sum(jnp.where(rows_lanes == EXPERTS, table, 0.0), axis=1, keepdims=True)
        gate = accg[...] * scale
        act[half] = (jax.nn.silu(gate) * (accu[...] * scale) * weight).astype(BF)

    gate_up(core)
    activate(core)
    table_waits[-1]()
    for wait in forwards:
        wait()
    gate_up(sibling)
    activate(sibling)
    for copy in wd_loads:
        copy.wait()

    def down(half, target, q):
        for start in range(0, Q, 256):
            product = jnp.dot(act[half], wd[q, :, start:start + 256], preferred_element_type=F32).astype(BF)
            target[:, :, :, :, q // 2, q % 2, :, start:start + 256] = product.reshape(2, 2, 2, 2, 16, 256)

    waits = []
    for q in range(4):
        down(sibling, sh, q)
        where = (EVERY,) * 4 + (q // 2, q % 2)
        waits.append(sems.remote(sh.at[where], rhc.at[where], rhc.at[where], partner["core"]))
    for q in range(4):
        down(core, ah, q)
    for q in range(4):
        waits[q]()
        where = (EVERY,) * 4 + (q // 2, q % 2)
        ah[where] = ah[where] + rhc[where]
    last = reduce_scatter(ah, rh, C_DIMS, C_BITS, C_PARTS)
    for (start, width), mine, other in last:
        columns = pl.ds(start, width)
        outs[:, columns] = hid[:, columns] + (ah[mine].astype(F32) + rh[other].astype(F32))

    for j in range(4):
        fsend[j // 2, j % 2] = outs[4 * j:4 * j + 4, :]
    waits = [
        sems.remote(fsend.at[p1, p0], frecv.at[x1, x0], frecv.at[p1, p0], partner[name])
        for name, p1, p0 in lines
    ]
    frecv[x1, x0] = fsend[x1, x0]
    for wait in waits:
        wait()
    for j in range(4):
        out_ref[:, j * Q:(j + 1) * Q] = frecv[j // 2, j % 2].astype(BF)
    assert sems.count <= SEMS
    for copy in sems.pending:
        copy.wait_send()


def layer(rel, residual, weights, value_weight, w_out, w_gate, w_up, w_down):
    vmem = pl.BlockSpec(memory_space=pltpu.VMEM)
    hbm = pl.BlockSpec(memory_space=pl.ANY)
    b_shape, c_shape = (2,) * 5 + (16, Q), (2,) * 6 + (16, Q)
    return pl.pallas_call(
        kernel,
        out_shape=jax.ShapeDtypeStruct((4, D), BF),
        in_specs=[vmem] * 4 + [hbm] * 4,
        out_specs=vmem,
        scratch_shapes=[
            pltpu.VMEM((4, HEAD, Q), BF),
            pltpu.VMEM((4, Q, FF), BF),
            pltpu.VMEM((4, Q, FF), BF),
            pltpu.VMEM((4, FF, Q), BF),
            pltpu.VMEM((2, 2, 4, Q), F32),
            pltpu.VMEM((2, 2, 4, 128), F32),
            pltpu.VMEM((16, Q), F32),
            pltpu.VMEM(b_shape, BF),
            pltpu.VMEM(b_shape, BF),
            pltpu.VMEM(b_shape, BF),
            pltpu.VMEM(b_shape, BF),
            pltpu.VMEM((3, 16, 128), F32),
            pltpu.VMEM((2, 16, 128), F32),
            pltpu.VMEM((2,) * 5 + (16, 128), F32),
            pltpu.VMEM((2,) + c_shape, BF),
            pltpu.VMEM((256, FF), F32),
            pltpu.VMEM((256, FF), F32),
            pltpu.VMEM((2, 256, FF), BF),
            pltpu.VMEM(c_shape, BF),
            pltpu.VMEM(c_shape, BF),
            pltpu.VMEM(c_shape, BF),
            pltpu.VMEM(c_shape, BF),
            pltpu.VMEM((16, Q), F32),
            pltpu.VMEM((2, 2, 4, Q), F32),
            pltpu.VMEM((2, 2, 4, Q), F32),
            pltpu.SemaphoreType.DMA((10,)),
            pltpu.SemaphoreType.DMA((SEMS,)),
            pltpu.SemaphoreType.DMA((SEMS,)),
        ],
        compiler_params=pltpu.CompilerParams(
            collective_id=0, has_side_effects=True, vmem_limit_bytes=58 * 2**20
        ),
    )(rel, residual, weights, value_weight, w_out, w_gate, w_up, w_down)


def local(
    queries, latent_cache, cache_lengths, residual, expert_ids, route_weights,
    value_weight, w_out, w_gate, w_up, w_down,
):
    role = lax.axis_index("role")
    latents = attend(queries, latent_cache, cache_lengths)
    relocated = lax.all_to_all(latents, "dev", split_axis=1, concat_axis=0, tiled=True)
    by_place = relocated.reshape(2, 4, 4, 2, 4, KEY_VALUE_RANK)
    by_place = jnp.where(role == 0, by_place, by_place[::-1])

    def gray(array, axis):
        picks = [lax.slice_in_dim(array, at, at + 1, axis=axis) for at in (0, 1, 3, 2)]
        return jnp.concatenate(picks, axis)

    by_place = gray(gray(by_place, 1), 2)
    rel = by_place.transpose(3, 0, 1, 2, 4, 5).reshape(2, 128, KEY_VALUE_RANK)
    onehot = expert_ids[:, :, None] == jnp.arange(128, dtype=jnp.int32)[None, None, :]
    weights = jnp.sum(jnp.where(onehot, route_weights[:, :, None], 0.0), 1)
    by_quarter = residual.astype(F32).reshape(4, 2, 2, Q).transpose(1, 2, 0, 3)
    return layer(
        rel, by_quarter, weights, value_weight[0], w_out,
        w_gate.reshape(4, Q, FF), w_up.reshape(4, Q, FF), w_down[0],
    )


def solution(mesh):
    return jax.shard_map(
        local,
        mesh=mesh,
        in_specs=(
            P(("role", "dev"), None, None),
            P(("role", "dev"), None, None),
            P(("role", "dev")),
            P(("role", "dev"), None),
            P(("role", "dev"), None),
            P(("role", "dev"), None),
            P("dev", None, None),
            P("dev", None),
            P(("role", "dev"), None, None),
            P(("role", "dev"), None, None),
            P(("role", "dev"), None, None),
        ),
        out_specs=P(("role", "dev"), None),
        check_vma=False,
    )
```

```python
import math

import jax
import jax.numpy as jnp
from jax import lax
from jax.experimental import pallas as pl
from jax.experimental.pallas import tpu as pltpu
from jax.sharding import PartitionSpec as P

KEY_VALUE_RANK = 512
HEADS = 64
LEN = 512
LATENT = 576
EXPERTS = 16
MESH = pl.DeviceIdType.MESH
D = 7168
Q = D // 4
FF = 256
HEAD = 128
BF = jnp.bfloat16
F32 = jnp.float32
score_scale = 1.0 / math.sqrt(192.0)


def parts_of(tiles):
    offset, parts = 0, []
    for count in tiles:
        parts.append((offset * 128, count * 128))
        offset += count
    assert offset * 128 == Q
    return parts


B_PARTS = parts_of((3, 3, 3, 3, 2))
B_BITS = ("x1", "y1", "z0", "x0", "y0")
C_PARTS = parts_of((3, 2, 2, 3, 2, 2))
C_BITS = ("x1", "y1", "z1", "x0", "y0", "z0")
B_DIMS = ("z0", "y1", "y0", "x1", "x0")
C_DIMS = ("z1",) + B_DIMS
T_DIMS = ("z1", "z0", "y1", "y0")
EVERY = slice(None)


class Sems:
    def __init__(self, sends, recvs):
        self.sends, self.recvs, self.count, self.pending = sends, recvs, 0, []

    def remote(self, source, target, landing, device):
        n = self.count
        self.count += 1
        copy = pltpu.make_async_remote_copy(
            src_ref=source,
            dst_ref=target,
            send_sem=self.sends.at[n],
            recv_sem=self.recvs.at[n],
            device_id=device,
            device_id_type=MESH,
        )
        copy.start()
        self.pending.append(copy)
        return pltpu.make_async_remote_copy(
            src_ref=source,
            dst_ref=landing,
            send_sem=self.sends.at[n],
            recv_sem=self.recvs.at[n],
            device_id=device,
            device_id_type=MESH,
        ).wait_recv


SEMS = 136


def kernel(
    len_ref, res_ref, ids_ref, rw_ref, vw_ref, q_hbm, cache_hbm, wo_hbm, wg_hbm, wu_hbm, wd_hbm, out_ref,
    qv, cv, lat, mbuf, lbuf, rel, resq, wts, a2a, wo, wg, wu, wd, resx, wx, hid, sb, ab, rbc, rb, ss, ssr, tab, g, accg, accu, act,
    sh, ah, rhc, rh, outs, fsend, frecv, loads, sends, recvs,
):
    role, dev = lax.axis_index("role"), lax.axis_index("dev")
    core, x, y, zl = dev % 2, (dev // 2) % 4, (dev // 8) % 4, dev // 32
    own = {
        "x1": x // 2, "x0": (x + x // 2) % 2, "y1": y // 2, "y0": (y + y // 2) % 2,
        "z1": role, "z0": (zl + role) % 2,
    }
    partner = {
        "core": (role, dev + 1 - 2 * core),
        "x1": (role, dev + 2 * (3 - 2 * x)),
        "x0": (role, dev + 2 * (1 - 2 * (x % 2))),
        "xd": (role, dev + 2 * ((x + 2) % 4 - x)),
        "y1": (role, dev + 8 * (3 - 2 * y)),
        "y0": (role, dev + 8 * (1 - 2 * (y % 2))),
        "z1": (1 - role, dev + 32 * (1 - 2 * zl)),
        "z0": (role, dev + 32 * (1 - 2 * zl)),
    }
    sibling = 1 - core

    fetch = []

    def load(source, target):
        copy = pltpu.make_async_copy(source, target, loads.at[len(fetch)])
        copy.start()
        fetch.append(copy)
        return copy

    attention_loads = [(load(q_hbm.at[n], qv.at[n]), load(cache_hbm.at[n], cv.at[n])) for n in range(4)]
    wo_loads = [load(wo_hbm.at[:, pl.ds(q * Q, Q)], wo.at[q]) for q in range(4)]
    wg_load, wu_load = load(wg_hbm, wg), load(wu_hbm, wu)
    wd_loads = [load(wd_hbm.at[:, pl.ds(q * Q, Q)], wd.at[q]) for q in range(4)]

    barrier = pltpu.get_barrier_semaphore()

    def greet(d, carry):
        pl.semaphore_signal(barrier, inc=1, device_id=(role, (dev + d) % HEADS), device_id_type=MESH)
        return carry

    lax.fori_loop(1, HEADS, greet, 0)
    pl.semaphore_signal(barrier, inc=1, device_id=partner["z1"], device_id_type=MESH)

    for q in range(4):
        resq[q // 2, q % 2] = res_ref[:, q * Q:(q + 1) * Q].astype(F32)
    four_lanes = lax.broadcasted_iota(jnp.int32, (4, 128), 1)
    dense = jnp.zeros((4, 128), F32)
    for k in range(8):
        dense = dense + jnp.where(four_lanes == ids_ref[:, k:k + 1], rw_ref[:, k:k + 1], 0.0)
    wts[...] = dense

    slots = lax.broadcasted_iota(jnp.int32, (HEADS, LEN), 1)
    for n in range(4):
        for copy in attention_loads[n]:
            copy.wait()
        scores = lax.dot_general(
            qv[n], cv[n], (((1,), (1,)), ((), ())), preferred_element_type=F32
        ) * score_scale
        scores = jnp.where(slots < len_ref[n], scores, -jnp.inf)
        raised = jnp.exp(scores - jnp.max(scores, axis=1, keepdims=True))
        chances = (raised / jnp.sum(raised, axis=1, keepdims=True)).astype(BF)
        lat[n] = jnp.dot(chances, cv[n, :, :KEY_VALUE_RANK], preferred_element_type=F32).astype(BF)

    to = lax.broadcasted_iota(jnp.int32, (256, 256), 0)
    source = lax.broadcasted_iota(jnp.int32, (256, 256), 1)
    regroup = jnp.where(source == (to % 16) * 16 + to // 16, 1.0, 0.0).astype(BF)
    for group in range(4):
        heads = slice(16 * group, 16 * group + 16)
        pieces = [lat[n, heads, 128 * c:128 * c + 128] for c in range(4) for n in range(4)]
        moved = jnp.dot(regroup, jnp.concatenate(pieces, axis=0), preferred_element_type=F32)
        mbuf[heads] = moved.astype(BF).reshape(16, 16, 128)

    pl.semaphore_wait(barrier, HEADS)
    seat = (((core * 2 + own["z0"]) * 2 + own["y1"]) * 2 + own["y0"]) * 4 + own["x1"] * 2 + own["x0"]

    def message(head):
        return pltpu.make_async_remote_copy(
            src_ref=mbuf.at[head], dst_ref=lbuf.at[seat], send_sem=a2a.at[0], recv_sem=a2a.at[1],
            device_id=(role, head), device_id_type=MESH,
        )

    def post(d, carry):
        message((dev + d) % HEADS).start()
        return carry

    lax.fori_loop(1, HEADS, post, 0)
    lbuf[seat] = mbuf[dev]

    sems = Sems(sends, recvs)
    x1, x0 = own["x1"], own["x0"]
    lines = (("x0", x1, 1 - x0), ("x1", 1 - x1, x0), ("xd", 1 - x1, 1 - x0))

    arrivals = []
    for name, p1, p0 in lines:
        arrivals.append(sems.remote(resq.at[p1, p0], resx.at[x1, x0], resx.at[p1, p0], partner[name]))
        arrivals.append(sems.remote(wts, wx.at[x1, x0], wx.at[p1, p0], partner[name]))
    resx[x1, x0] = resq[x1, x0]
    wx[x1, x0] = wts[...]

    spread = jnp.where(source == ((to % 64) // 4) * 16 + (to // 64) * 4 + to % 4, 1.0, 0.0).astype(BF)
    everyone = pltpu.make_async_remote_copy(
        src_ref=mbuf.at[pl.ds(0, HEADS - 1)], dst_ref=lbuf.at[pl.ds(0, HEADS - 1)],
        send_sem=a2a.at[0], recv_sem=a2a.at[1], device_id=partner["core"], device_id_type=MESH,
    )
    everyone.wait_recv()
    for group in range(4):
        rows = lbuf[16 * group:16 * group + 16].reshape(256, 128)
        moved = jnp.dot(spread, rows, preferred_element_type=F32).astype(BF)
        for c in range(4):
            rel[group // 2, 64 * (group % 2):64 * (group % 2) + 64, 128 * c:128 * c + 128] = moved[64 * c:64 * c + 64]

    for copy in wo_loads:
        copy.wait()

    def project(half, target):
        values = jnp.dot(rel[half], vw_ref[...], preferred_element_type=F32).astype(BF)

        def quarter(q):
            product = jnp.dot(values, wo[q], preferred_element_type=F32).astype(BF)
            target[:, :, :, q // 2, q % 2] = product.reshape(2, 2, 2, 16, Q)

        return quarter

    quarter = project(sibling, sb)
    waits = []
    for q in range(4):
        quarter(q)
        where = (EVERY, EVERY, EVERY, q // 2, q % 2)
        waits.append(sems.remote(sb.at[where], rbc.at[where], rbc.at[where], partner["core"]))
    quarter = project(core, ab)
    for q in range(4):
        quarter(q)
    for q in range(4):
        waits[q]()
        where = (EVERY, EVERY, EVERY, q // 2, q % 2)
        ab[where] = ab[where] + rbc[where]

    def reduce_scatter(buf, landing, dims, bits, parts):
        number = len(bits)
        waits = {}

        def place(k, step, current):
            order = [bits[(k + j) % number] for j in range(number)]
            indices = []
            for dim in dims:
                at = order.index(dim)
                if at < step:
                    indices.append(own[dim])
                elif at == step:
                    indices.append(own[dim] if current else 1 - own[dim])
                else:
                    indices.append(EVERY)
            return tuple(indices) + (EVERY, pl.ds(*parts[k])), order[step]

        for step in range(number):
            for k in range(len(parts)):
                if step:
                    waits[k]()
                    mine, _ = place(k, step - 1, True)
                    other, _ = place(k, step - 1, False)
                    buf[mine] = buf[mine] + landing[other]
                mine, bit = place(k, step, True)
                other, _ = place(k, step, False)
                waits[k] = sems.remote(buf.at[other], landing.at[mine], landing.at[other], partner[bit])
        last = []
        for k in range(len(parts)):
            waits[k]()
            mine, _ = place(k, number - 1, True)
            other, _ = place(k, number - 1, False)
            last.append((parts[k], mine, other))
        return last

    last = reduce_scatter(ab, rb, B_DIMS, B_BITS, B_PARTS)

    for wait in arrivals:
        wait()
    for j in range(4):
        hid[4 * j:4 * j + 4, :] = resx[j // 2, j % 2]
    block = tuple(own[dim] for dim in C_DIMS)
    squares = jnp.zeros((16, 1), F32)
    for (start, width), mine, other in last:
        columns = pl.ds(start, width)
        total = hid[:, columns] + (ab[mine].astype(F32) + rb[other].astype(F32))
        rounded = total.astype(BF)
        g[(core,) + block + (EVERY, columns)] = rounded
        total = rounded.astype(F32)
        hid[:, columns] = total
        squares = squares + jnp.sum(total * total, axis=1, keepdims=True)
    ss[0] = jnp.broadcast_to(squares, (16, 128))

    def gather_place(k, step, mine, bits, dims):
        number = len(bits)
        order = [bits[(k + number - 1 - j) % number] for j in range(number)]
        indices = []
        for dim in dims:
            at = order.index(dim)
            if at < step:
                indices.append(EVERY)
            elif at == step:
                indices.append(own[dim] if mine else 1 - own[dim])
            else:
                indices.append(own[dim])
        return tuple(indices), order[step]

    waits, forwards = {}, []
    table_waits = []
    t_bits = ("y0", "y1", "z0", "z1")
    lanes = lax.broadcasted_iota(jnp.int32, (16, 128), 1)
    steps = len(C_BITS)
    for step in range(steps + 1):
        for k in range(len(C_PARTS)):
            tail = (EVERY, pl.ds(*C_PARTS[k]))
            if step:
                waits[k]()
            if step < steps:
                mine, bit = gather_place(k, step, True, C_BITS, C_DIMS)
                other, _ = gather_place(k, step, False, C_BITS, C_DIMS)
                here = g.at[(core,) + mine + tail]
                waits[k] = sems.remote(here, here, g.at[(core,) + other + tail], partner[bit])
            if step >= steps - 1:
                mine, _ = gather_place(k, steps - 1, step == steps - 1, C_BITS, C_DIMS)
                here = g.at[(core,) + mine + tail]
                forwards.append(sems.remote(here, here, g.at[(sibling,) + mine + tail], partner["core"]))
        if step < 2:
            table_waits.append(sems.remote(ss.at[step], ssr.at[step], ssr.at[step], partner[("x0", "x1")[step]]))
            table_waits[-1]()
            ss[step + 1] = ss[step] + ssr[step]
            if step == 1:
                weights = jnp.concatenate([wx[j // 2, j % 2] for j in range(4)], axis=0)
                scale = lax.rsqrt(ss[2] * (1.0 / D) + 1e-06)
                tab[(core,) + tuple(own[dim] for dim in T_DIMS)] = jnp.where(lanes == EXPERTS, scale, weights)
        elif step < 6:
            if step > 2:
                table_waits[-1]()
            mine, bit = gather_place(3, step - 2, True, t_bits, T_DIMS)
            other, _ = gather_place(3, step - 2, False, t_bits, T_DIMS)
            here = tab.at[(core,) + mine]
            table_waits.append(sems.remote(here, here, tab.at[(core,) + other], partner[bit]))
        else:
            table_waits[-1]()
            table_waits.append(sems.remote(tab.at[core], tab.at[core], tab.at[sibling], partner["core"]))

    wg_load.wait()
    wu_load.wait()
    expert = role * 8 + zl * 4 + y
    rows_lanes = lax.broadcasted_iota(jnp.int32, (256, 128), 1)

    def gate_up(half):
        accg[...] = jnp.zeros_like(accg)
        accu[...] = jnp.zeros_like(accu)

        def quarter(q, carry):
            rows = g[half, :, :, :, :, q // 2, q % 2].reshape(256, Q)
            accg[...] += jnp.dot(rows, wg[q], preferred_element_type=F32)
            accu[...] += jnp.dot(rows, wu[q], preferred_element_type=F32)
            return carry

        lax.fori_loop(0, 4, quarter, 0)

    def activate(half):
        table = tab[half].reshape(256, 128)
        weight = jnp.sum(jnp.where(rows_lanes == expert, table, 0.0), axis=1, keepdims=True)
        scale = jnp.sum(jnp.where(rows_lanes == EXPERTS, table, 0.0), axis=1, keepdims=True)
        gate = accg[...] * scale
        act[half] = (jax.nn.silu(gate) * (accu[...] * scale) * weight).astype(BF)

    gate_up(core)
    activate(core)
    table_waits[-1]()
    for wait in forwards:
        wait()
    gate_up(sibling)
    activate(sibling)
    for copy in wd_loads:
        copy.wait()

    def down(half, target, q):
        for start in range(0, Q, 256):
            product = jnp.dot(act[half], wd[q, :, start:start + 256], preferred_element_type=F32).astype(BF)
            target[:, :, :, :, q // 2, q % 2, :, start:start + 256] = product.reshape(2, 2, 2, 2, 16, 256)

    waits = []
    for q in range(4):
        down(sibling, sh, q)
        where = (EVERY,) * 4 + (q // 2, q % 2)
        waits.append(sems.remote(sh.at[where], rhc.at[where], rhc.at[where], partner["core"]))
    for q in range(4):
        down(core, ah, q)
    for q in range(4):
        waits[q]()
        where = (EVERY,) * 4 + (q // 2, q % 2)
        ah[where] = ah[where] + rhc[where]
    last = reduce_scatter(ah, rh, C_DIMS, C_BITS, C_PARTS)
    for (start, width), mine, other in last:
        columns = pl.ds(start, width)
        outs[:, columns] = hid[:, columns] + (ah[mine].astype(F32) + rh[other].astype(F32))

    for j in range(4):
        fsend[j // 2, j % 2] = outs[4 * j:4 * j + 4, :]
    waits = [
        sems.remote(fsend.at[p1, p0], frecv.at[x1, x0], frecv.at[p1, p0], partner[name])
        for name, p1, p0 in lines
    ]
    frecv[x1, x0] = fsend[x1, x0]
    for wait in waits:
        wait()
    for j in range(4):
        out_ref[:, j * Q:(j + 1) * Q] = frecv[j // 2, j % 2].astype(BF)
    assert sems.count <= SEMS
    everyone.wait_send()
    for copy in sems.pending:
        copy.wait_send()


def layer(*operands):
    vmem = pl.BlockSpec(memory_space=pltpu.VMEM)
    hbm = pl.BlockSpec(memory_space=pl.ANY)
    b_shape, c_shape = (2,) * 5 + (16, Q), (2,) * 6 + (16, Q)
    return pl.pallas_call(
        kernel,
        out_shape=jax.ShapeDtypeStruct((4, D), BF),
        in_specs=[pl.BlockSpec(memory_space=pltpu.SMEM)] + [vmem] * 4 + [hbm] * 6,
        out_specs=vmem,
        scratch_shapes=[
            pltpu.VMEM((4, HEADS, LATENT), BF),
            pltpu.VMEM((4, LEN, LATENT), BF),
            pltpu.VMEM((4, HEADS, KEY_VALUE_RANK), BF),
            pltpu.VMEM((HEADS, 16, 128), BF),
            pltpu.VMEM((HEADS, 16, 128), BF),
            pltpu.VMEM((2, 128, KEY_VALUE_RANK), BF),
            pltpu.VMEM((2, 2, 4, Q), F32),
            pltpu.VMEM((4, 128), F32),
            pltpu.SemaphoreType.DMA((2,)),
            pltpu.VMEM((4, HEAD, Q), BF),
            pltpu.VMEM((4, Q, FF), BF),
            pltpu.VMEM((4, Q, FF), BF),
            pltpu.VMEM((4, FF, Q), BF),
            pltpu.VMEM((2, 2, 4, Q), F32),
            pltpu.VMEM((2, 2, 4, 128), F32),
            pltpu.VMEM((16, Q), F32),
            pltpu.VMEM(b_shape, BF),
            pltpu.VMEM(b_shape, BF),
            pltpu.VMEM(b_shape, BF),
            pltpu.VMEM(b_shape, BF),
            pltpu.VMEM((3, 16, 128), F32),
            pltpu.VMEM((2, 16, 128), F32),
            pltpu.VMEM((2,) * 5 + (16, 128), F32),
            pltpu.VMEM((2,) + c_shape, BF),
            pltpu.VMEM((256, FF), F32),
            pltpu.VMEM((256, FF), F32),
            pltpu.VMEM((2, 256, FF), BF),
            pltpu.VMEM(c_shape, BF),
            pltpu.VMEM(c_shape, BF),
            pltpu.VMEM(c_shape, BF),
            pltpu.VMEM(c_shape, BF),
            pltpu.VMEM((16, Q), F32),
            pltpu.VMEM((2, 2, 4, Q), F32),
            pltpu.VMEM((2, 2, 4, Q), F32),
            pltpu.SemaphoreType.DMA((18,)),
            pltpu.SemaphoreType.DMA((SEMS,)),
            pltpu.SemaphoreType.DMA((SEMS,)),
        ],
        compiler_params=pltpu.CompilerParams(
            collective_id=0, has_side_effects=True, vmem_limit_bytes=58 * 2**20
        ),
    )(*operands)


def local(
    queries, latent_cache, cache_lengths, residual, expert_ids, route_weights,
    value_weight, w_out, w_gate, w_up, w_down,
):
    return layer(
        cache_lengths, residual, expert_ids, route_weights, value_weight[0], queries, latent_cache, w_out,
        w_gate.reshape(4, Q, FF), w_up.reshape(4, Q, FF), w_down[0],
    )


def solution(mesh):
    return jax.shard_map(
        local,
        mesh=mesh,
        in_specs=(
            P(("role", "dev"), None, None),
            P(("role", "dev"), None, None),
            P(("role", "dev")),
            P(("role", "dev"), None),
            P(("role", "dev"), None),
            P(("role", "dev"), None),
            P("dev", None, None),
            P("dev", None),
            P(("role", "dev"), None, None),
            P(("role", "dev"), None, None),
            P(("role", "dev"), None, None),
        ),
        out_specs=P(("role", "dev"), None),
        check_vma=False,
    )
```

```python
import math

import jax
import jax.numpy as jnp
from jax import lax
from jax.experimental import pallas as pl
from jax.experimental.pallas import tpu as pltpu
from jax.sharding import PartitionSpec as P

KEY_VALUE_RANK = 512
HEADS = 64
LEN = 512
LATENT = 576
EXPERTS = 16
MESH = pl.DeviceIdType.MESH
D = 7168
Q = D // 4
FF = 256
HEAD = 128
BF = jnp.bfloat16
F32 = jnp.float32
score_scale = 1.0 / math.sqrt(192.0)


B_DIMS = ("z0", "y1", "y0", "x1", "x0")
C_DIMS = ("z1",) + B_DIMS
HALF = Q // 2
B_GROUPS = ((("x1", "y1"), ("x0", "y0", "z0")), (("x0", "y0"), ("x1", "y1", "z0")))
B_PIECES = ((0, 2, 0), (4, 2, 1), (2, 2, 0), (6, 1, 1))
C_GROUPS = ((("x1", "y1", "z1"), ("x0", "y0", "z0")), (("x0", "y0", "z0"), ("x1", "y1", "z1")))
C_PIECES = ((0, 2, 0), (3, 1, 1), (5, 1, 2), (2, 1, 0), (4, 1, 1), (6, 1, 2))


def all_pieces(groups, pieces):
    found = []
    for tile, count, turn in pieces:
        for at, (ring, _) in enumerate(groups):
            columns = pl.ds(at * HALF + tile * 128, count * 128)
            found.append((at, columns, ring[turn:] + ring[:turn]))
    return found


def subsets(bits):
    found = [tuple(bit for i, bit in enumerate(bits) if n >> i & 1) for n in range(1, 2 ** len(bits))]
    return sorted(found, key=lambda flips: -len(flips))


EVERY = slice(None)


class Sems:
    def __init__(self, sends, recvs):
        self.sends, self.recvs, self.count, self.pending = sends, recvs, 0, []

    def remote(self, source, target, landing, device):
        n = self.count
        self.count += 1
        copy = pltpu.make_async_remote_copy(
            src_ref=source,
            dst_ref=target,
            send_sem=self.sends.at[n],
            recv_sem=self.recvs.at[n],
            device_id=device,
            device_id_type=MESH,
        )
        copy.start()
        self.pending.append(copy)
        return pltpu.make_async_remote_copy(
            src_ref=source,
            dst_ref=landing,
            send_sem=self.sends.at[n],
            recv_sem=self.recvs.at[n],
            device_id=device,
            device_id_type=MESH,
        ).wait_recv


SEMS = 200


def kernel(
    len_ref, res_ref, ids_ref, rw_ref, vw_ref, q_hbm, cache_hbm, wo_hbm, wg_hbm, wu_hbm, wd_hbm, out_ref,
    qv, cv, lat, mbuf, lbuf, rel, resq, wts, a2a, wo, wg, wu, wd, resx, wx, hid, values, sb, ab, rbc, rb, ss, ssr, tab, g, accg, accu, act,
    sh, ah, rhc, rh, outs, fsend, frecv, loads, sends, recvs,
):
    role, dev = lax.axis_index("role"), lax.axis_index("dev")
    core, x, y, zl = dev % 2, (dev // 2) % 4, (dev // 8) % 4, dev // 32
    own = {
        "x1": x // 2, "x0": (x + x // 2) % 2, "y1": y // 2, "y0": (y + y // 2) % 2,
        "z1": role, "z0": (zl + role) % 2,
    }
    def across(*flips):
        at = {bit: 1 - own[bit] if bit in flips else own[bit] for bit in own}
        to_x = 2 * at["x1"] + (at["x1"] + at["x0"]) % 2
        to_y = 2 * at["y1"] + (at["y1"] + at["y0"]) % 2
        to_zl = (at["z1"] + at["z0"]) % 2
        return at["z1"], ((to_zl * 4 + to_y) * 4 + to_x) * 2 + core

    twin = (role, dev + 1 - 2 * core)
    sibling = 1 - core

    fetch = []

    def load(source, target):
        copy = pltpu.make_async_copy(source, target, loads.at[len(fetch)])
        copy.start()
        fetch.append(copy)
        return copy

    attention_loads = [(load(q_hbm.at[n], qv.at[n]), load(cache_hbm.at[n], cv.at[n])) for n in range(4)]
    wo_loads = [load(wo_hbm.at[:, pl.ds(q * Q, Q)], wo.at[q]) for q in range(4)]
    wg_load, wu_load = load(wg_hbm, wg), load(wu_hbm, wu)
    wd_loads = [load(wd_hbm.at[:, pl.ds(q * Q, Q)], wd.at[q]) for q in range(4)]

    barrier = pltpu.get_barrier_semaphore()

    def greet(d, carry):
        pl.semaphore_signal(barrier, inc=1, device_id=(role, (dev + d) % HEADS), device_id_type=MESH)
        return carry

    lax.fori_loop(1, HEADS, greet, 0)
    beyond = [across(*flips) for flips in subsets(("x1", "y1", "z1")) if "z1" in flips]
    for device in beyond:
        pl.semaphore_signal(barrier, inc=1, device_id=device, device_id_type=MESH)

    for q in range(4):
        resq[q // 2, q % 2] = res_ref[:, q * Q:(q + 1) * Q].astype(F32)
    four_lanes = lax.broadcasted_iota(jnp.int32, (4, 128), 1)
    dense = jnp.zeros((4, 128), F32)
    for k in range(8):
        dense = dense + jnp.where(four_lanes == ids_ref[:, k:k + 1], rw_ref[:, k:k + 1], 0.0)
    wts[...] = dense

    slots = lax.broadcasted_iota(jnp.int32, (HEADS, LEN), 1)
    for pair in attention_loads:
        for copy in pair:
            copy.wait()
    scores = [jnp.dot(qv[n], cv[n], preferred_element_type=F32) * score_scale for n in range(4)]
    for n in range(4):
        live = jnp.where(slots < len_ref[n], scores[n], -jnp.inf)
        raised = jnp.exp(live - jnp.max(live, axis=1, keepdims=True))
        chances = (raised / jnp.sum(raised, axis=1, keepdims=True)).astype(BF)
        lat[n] = lax.dot_general(
            chances, cv[n, :KEY_VALUE_RANK, :], (((1,), (1,)), ((), ())), preferred_element_type=F32
        ).astype(BF)

    to = lax.broadcasted_iota(jnp.int32, (256, 256), 0)
    source = lax.broadcasted_iota(jnp.int32, (256, 256), 1)
    regroup = jnp.where(source == (to % 16) * 16 + to // 16, 1.0, 0.0).astype(BF)
    for group in range(4):
        heads = slice(16 * group, 16 * group + 16)
        pieces = [lat[n, heads, 128 * c:128 * c + 128] for c in range(4) for n in range(4)]
        moved = jnp.dot(regroup, jnp.concatenate(pieces, axis=0), preferred_element_type=F32)
        mbuf[heads] = moved.astype(BF).reshape(16, 16, 128)

    pl.semaphore_wait(barrier, HEADS - 1 + len(beyond))
    seat = (((core * 2 + own["z0"]) * 2 + own["y1"]) * 2 + own["y0"]) * 4 + own["x1"] * 2 + own["x0"]

    def message(head):
        return pltpu.make_async_remote_copy(
            src_ref=mbuf.at[head], dst_ref=lbuf.at[seat], send_sem=a2a.at[0], recv_sem=a2a.at[1],
            device_id=(role, head), device_id_type=MESH,
        )

    def post(d, carry):
        message((dev + d) % HEADS).start()
        return carry

    lax.fori_loop(1, HEADS, post, 0)
    lbuf[seat] = mbuf[dev]

    sems = Sems(sends, recvs)
    x1, x0 = own["x1"], own["x0"]
    lines = (
        (across("x1", "x0"), 1 - x1, 1 - x0), (across("x1"), 1 - x1, x0), (across("x0"), x1, 1 - x0),
    )

    arrivals = []
    for device, p1, p0 in lines:
        arrivals.append(sems.remote(resq.at[p1, p0], resx.at[x1, x0], resx.at[p1, p0], device))
        arrivals.append(sems.remote(wts, wx.at[x1, x0], wx.at[p1, p0], device))
    resx[x1, x0] = resq[x1, x0]
    wx[x1, x0] = wts[...]

    spread = jnp.where(source == ((to % 64) // 4) * 16 + (to // 64) * 4 + to % 4, 1.0, 0.0).astype(BF)
    everyone = pltpu.make_async_remote_copy(
        src_ref=mbuf.at[pl.ds(0, HEADS - 1)], dst_ref=lbuf.at[pl.ds(0, HEADS - 1)],
        send_sem=a2a.at[0], recv_sem=a2a.at[1], device_id=twin, device_id_type=MESH,
    )
    everyone.wait_recv()
    for group in range(4):
        rows = lbuf[16 * group:16 * group + 16].reshape(256, 128)
        moved = jnp.dot(spread, rows, preferred_element_type=F32).astype(BF)
        for c in range(4):
            rel[group // 2, 64 * (group % 2):64 * (group % 2) + 64, 128 * c:128 * c + 128] = moved[64 * c:64 * c + 64]

    def reduce_scatter(produce, given, taken, buf, landing, dims, groups, pieces):
        whole = (EVERY,) * (len(dims) + 1)
        found = all_pieces(groups, pieces)
        waits = [None] * len(found)

        def place(order, step, mine):
            indices = []
            for dim in dims:
                at = order.index(dim) if dim in order else len(order)
                here = own[dim] if mine else 1 - own[dim]
                indices.append(own[dim] if at < step else here if at == step else EVERY)
            return tuple(indices) + (EVERY,)

        def advance(n, step):
            _, columns, order = found[n]
            mine, other = place(order, step, True) + (columns,), place(order, step, False) + (columns,)
            if step < len(order):
                waits[n] = sems.remote(buf.at[other], landing.at[mine], landing.at[other], across(order[step]))

        def add(n, step):
            _, columns, order = found[n]
            waits[n]()
            if step < 0:
                buf[whole + (columns,)] = buf[whole + (columns,)] + taken[whole + (columns,)]
            else:
                mine, other = place(order, step, True) + (columns,), place(order, step, False) + (columns,)
                buf[mine] = buf[mine] + landing[other]

        for n, (_, columns, _) in enumerate(found):
            produce(sibling, given, columns)
            where = whole + (columns,)
            waits[n] = sems.remote(given.at[where], taken.at[where], taken.at[where], twin)
            produce(core, buf, columns)
            if n:
                add(n - 1, -1)
                advance(n - 1, 0)
        add(len(found) - 1, -1)
        advance(len(found) - 1, 0)
        rounds = len(groups[0][0])
        for step in range(1, rounds):
            for n in range(len(found)):
                add(n, step - 1)
                advance(n, step)
        result, last = [], []
        for at, (ring, direct) in enumerate(groups):
            columns = pl.ds(at * HALF, HALF)
            for n in range(len(found)):
                if found[n][0] == at:
                    add(n, rounds - 1)
            mine = tuple(own[dim] for dim in dims) + (EVERY, columns)
            others = []
            for flips in subsets(direct):
                other = tuple(1 - own[dim] if dim in flips else own[dim] for dim in dims) + (EVERY, columns)
                last.append(sems.remote(buf.at[other], landing.at[mine], landing.at[other], across(*flips)))
                others.append(other)
            result.append((columns, mine, others))
        for wait in last:
            wait()
        return result

    for copy in wo_loads:
        copy.wait()
    for half in range(2):
        values[half] = jnp.dot(rel[half], vw_ref[...], preferred_element_type=F32).astype(BF)

    def project(half, target, columns):
        weight = jnp.concatenate([wo[q, :, columns] for q in range(4)], axis=1)
        product = jnp.dot(values[half], weight, preferred_element_type=F32).astype(BF)
        width = columns.size
        for q in range(4):
            block = product[:, q * width:(q + 1) * width].reshape(2, 2, 2, 16, width)
            target[:, :, :, q // 2, q % 2, :, columns] = block

    summed = reduce_scatter(project, sb, rbc, ab, rb, B_DIMS, B_GROUPS, B_PIECES)

    for wait in arrivals:
        wait()
    for j in range(4):
        hid[4 * j:4 * j + 4, :] = resx[j // 2, j % 2]
    block = tuple(own[dim] for dim in C_DIMS)
    squares = jnp.zeros((16, 1), F32)
    for columns, mine, others in summed:
        total = ab[mine].astype(F32)
        for other in others:
            total = total + rb[other].astype(F32)
        rounded = (hid[:, columns] + total).astype(BF)
        g[(core,) + block + (EVERY, columns)] = rounded
        total = rounded.astype(F32)
        hid[:, columns] = total
        squares = squares + jnp.sum(total * total, axis=1, keepdims=True)

    direct_waits = []
    for at, (_, direct) in enumerate(C_GROUPS):
        columns = pl.ds(at * HALF, HALF)
        here = g.at[(core,) + block + (EVERY, columns)]
        waits = []
        for flips in subsets(direct):
            other = tuple(1 - own[dim] if dim in flips else own[dim] for dim in C_DIMS)
            waits.append(sems.remote(here, here, g.at[(core,) + other + (EVERY, columns)], across(*flips)))
        direct_waits.append(waits)

    ss[0] = jnp.broadcast_to(squares, (16, 128))
    square_waits = [
        sems.remote(ss.at[0], ssr.at[x1, x0], ssr.at[p1, p0], device) for device, p1, p0 in lines
    ]
    for wait in square_waits:
        wait()
    squares = ss[0]
    for _, p1, p0 in lines:
        squares = squares + ssr[p1, p0]
    weights = jnp.concatenate([wx[j // 2, j % 2] for j in range(4)], axis=0)
    lanes = lax.broadcasted_iota(jnp.int32, (16, 128), 1)
    scale = lax.rsqrt(squares * (1.0 / D) + 1e-06)
    table_at = (core, own["z1"], own["z0"], own["y1"], own["y0"])
    tab[table_at] = jnp.where(lanes == EXPERTS, scale, weights)

    def table_step(first, second, others):
        dims = ("z1", "z0", "y1", "y0")

        def at(flips):
            indices = []
            for dim in dims:
                if dim in (first, second):
                    indices.append(1 - own[dim] if dim in flips else own[dim])
                else:
                    indices.append(EVERY if others else own[dim])
            return (core,) + tuple(indices)

        return [
            sems.remote(tab.at[at(())], tab.at[at(())], tab.at[at(flips)], across(*flips))
            for flips in subsets((first, second))
        ]

    found = all_pieces(C_GROUPS, C_PIECES)
    waits, forwards = [None] * len(found), []

    def gather_place(n, step, mine):
        at, columns, order = found[n]
        indices = []
        for dim in C_DIMS:
            if dim not in order or order.index(dim) < step:
                indices.append(EVERY)
            elif order.index(dim) == step:
                indices.append(own[dim] if mine else 1 - own[dim])
            else:
                indices.append(own[dim])
        return tuple(indices) + (EVERY, columns)

    def forward(n, mine):
        where = gather_place(n, 2, mine)
        here = g.at[(core,) + where]
        forwards.append(sems.remote(here, here, g.at[(sibling,) + where], twin))

    table_waits = table_step("y0", "z0", False)
    for step in range(4):
        for n in range(len(found)):
            if step:
                waits[n]()
            elif n < 2:
                for wait in direct_waits[n]:
                    wait()
            if step < 3:
                here = g.at[(core,) + gather_place(n, step, True)]
                there = g.at[(core,) + gather_place(n, step, False)]
                waits[n] = sems.remote(here, here, there, across(found[n][2][step]))
            if step > 1:
                forward(n, step == 2)
        if step < 3:
            for wait in table_waits:
                wait()
        if step == 0:
            table_waits = table_step("y1", "z1", True)
        elif step == 1:
            table_waits = [sems.remote(tab.at[core], tab.at[core], tab.at[sibling], twin)]

    wg_load.wait()
    wu_load.wait()
    expert = role * 8 + zl * 4 + y
    rows_lanes = lax.broadcasted_iota(jnp.int32, (256, 128), 1)

    def gate_up(half):
        accg[...] = jnp.zeros_like(accg)
        accu[...] = jnp.zeros_like(accu)

        def quarter(q, carry):
            rows = g[half, :, :, :, :, q // 2, q % 2].reshape(256, Q)
            accg[...] += jnp.dot(rows, wg[q], preferred_element_type=F32)
            accu[...] += jnp.dot(rows, wu[q], preferred_element_type=F32)
            return carry

        lax.fori_loop(0, 4, quarter, 0)

    def activate(half):
        table = tab[half].reshape(256, 128)
        weight = jnp.sum(jnp.where(rows_lanes == expert, table, 0.0), axis=1, keepdims=True)
        scale = jnp.sum(jnp.where(rows_lanes == EXPERTS, table, 0.0), axis=1, keepdims=True)
        gate = accg[...] * scale
        act[half] = (jax.nn.silu(gate) * (accu[...] * scale) * weight).astype(BF)

    gate_up(core)
    activate(core)
    for wait in forwards:
        wait()
    gate_up(sibling)
    activate(sibling)
    for copy in wd_loads:
        copy.wait()

    def down(half, target, columns):
        weight = jnp.concatenate([wd[q, :, columns] for q in range(4)], axis=1)
        product = jnp.dot(act[half], weight, preferred_element_type=F32).astype(BF)
        width = columns.size
        for q in range(4):
            block = product[:, q * width:(q + 1) * width].reshape(2, 2, 2, 2, 16, width)
            target[:, :, :, :, q // 2, q % 2, :, columns] = block

    summed = reduce_scatter(down, sh, rhc, ah, rh, C_DIMS, C_GROUPS, C_PIECES)
    for columns, mine, others in summed:
        total = hid[:, columns] + ah[mine].astype(F32)
        for other in others:
            total = total + rh[other].astype(F32)
        outs[:, columns] = total

    for j in range(4):
        fsend[j // 2, j % 2] = outs[4 * j:4 * j + 4, :]
    waits = [
        sems.remote(fsend.at[p1, p0], frecv.at[x1, x0], frecv.at[p1, p0], device)
        for device, p1, p0 in lines
    ]
    frecv[x1, x0] = fsend[x1, x0]
    for wait in waits:
        wait()
    for j in range(4):
        out_ref[:, j * Q:(j + 1) * Q] = frecv[j // 2, j % 2].astype(BF)
    assert sems.count <= SEMS
    everyone.wait_send()
    for copy in sems.pending:
        copy.wait_send()


def layer(*operands):
    vmem = pl.BlockSpec(memory_space=pltpu.VMEM)
    hbm = pl.BlockSpec(memory_space=pl.ANY)
    b_shape, c_shape = (2,) * 5 + (16, Q), (2,) * 6 + (16, Q)
    return pl.pallas_call(
        kernel,
        out_shape=jax.ShapeDtypeStruct((4, D), BF),
        in_specs=[pl.BlockSpec(memory_space=pltpu.SMEM)] + [vmem] * 4 + [hbm] * 6,
        out_specs=vmem,
        scratch_shapes=[
            pltpu.VMEM((4, HEADS, LATENT), BF),
            pltpu.VMEM((4, LATENT, LEN), BF),
            pltpu.VMEM((4, HEADS, KEY_VALUE_RANK), BF),
            pltpu.VMEM((HEADS, 16, 128), BF),
            pltpu.VMEM((HEADS, 16, 128), BF),
            pltpu.VMEM((2, 128, KEY_VALUE_RANK), BF),
            pltpu.VMEM((2, 2, 4, Q), F32),
            pltpu.VMEM((4, 128), F32),
            pltpu.SemaphoreType.DMA((2,)),
            pltpu.VMEM((4, HEAD, Q), BF),
            pltpu.VMEM((4, Q, FF), BF),
            pltpu.VMEM((4, Q, FF), BF),
            pltpu.VMEM((4, FF, Q), BF),
            pltpu.VMEM((2, 2, 4, Q), F32),
            pltpu.VMEM((2, 2, 4, 128), F32),
            pltpu.VMEM((16, Q), F32),
            pltpu.VMEM((2, 128, HEAD), BF),
            pltpu.VMEM(b_shape, BF),
            pltpu.VMEM(b_shape, BF),
            pltpu.VMEM(b_shape, BF),
            pltpu.VMEM(b_shape, BF),
            pltpu.VMEM((1, 16, 128), F32),
            pltpu.VMEM((2, 2, 16, 128), F32),
            pltpu.VMEM((2,) * 5 + (16, 128), F32),
            pltpu.VMEM((2,) + c_shape, BF),
            pltpu.VMEM((256, FF), F32),
            pltpu.VMEM((256, FF), F32),
            pltpu.VMEM((2, 256, FF), BF),
            pltpu.VMEM(c_shape, BF),
            pltpu.VMEM(c_shape, BF),
            pltpu.VMEM(c_shape, BF),
            pltpu.VMEM(c_shape, BF),
            pltpu.VMEM((16, Q), F32),
            pltpu.VMEM((2, 2, 4, Q), F32),
            pltpu.VMEM((2, 2, 4, Q), F32),
            pltpu.SemaphoreType.DMA((18,)),
            pltpu.SemaphoreType.DMA((SEMS,)),
            pltpu.SemaphoreType.DMA((SEMS,)),
        ],
        compiler_params=pltpu.CompilerParams(
            collective_id=0, has_side_effects=True, vmem_limit_bytes=58 * 2**20
        ),
    )(*operands)


def local(
    queries, latent_cache, cache_lengths, residual, expert_ids, route_weights,
    value_weight, w_out, w_gate, w_up, w_down,
):
    return layer(
        cache_lengths, residual, expert_ids, route_weights, value_weight[0], queries, latent_cache.transpose(0, 2, 1), w_out,
        w_gate.reshape(4, Q, FF), w_up.reshape(4, Q, FF), w_down[0],
    )


def solution(mesh):
    return jax.shard_map(
        local,
        mesh=mesh,
        in_specs=(
            P(("role", "dev"), None, None),
            P(("role", "dev"), None, None),
            P(("role", "dev")),
            P(("role", "dev"), None),
            P(("role", "dev"), None),
            P(("role", "dev"), None),
            P("dev", None, None),
            P("dev", None),
            P(("role", "dev"), None, None),
            P(("role", "dev"), None, None),
            P(("role", "dev"), None, None),
        ),
        out_specs=P(("role", "dev"), None),
        check_vma=False,
    )
```

```python
import math

import jax
import jax.numpy as jnp
from jax import lax
from jax.experimental import pallas as pl
from jax.experimental.pallas import tpu as pltpu
from jax.sharding import PartitionSpec as P

KEY_VALUE_RANK = 512
HEADS = 64
CHIPS = HEADS // 2
LEN = 512
LATENT = 576
EXPERTS = 16
MESH = pl.DeviceIdType.MESH
D = 7168
Q = D // 4
FF = 256
HEAD = 128
BF = jnp.bfloat16
F32 = jnp.float32
score_scale = 1.0 / math.sqrt(192.0)


B_DIMS = ("z0", "y1", "y0", "x1", "x0")
C_DIMS = ("z1",) + B_DIMS
HALF = Q // 2
B_GROUPS = ((("x1", "y1"), ("x0", "y0", "z0")), (("x0", "y0"), ("x1", "y1", "z0")))
B_PIECES = ((0, 2, 0), (4, 2, 1), (2, 2, 0), (6, 1, 1))
C_GROUPS = ((("x1", "y1", "z1"), ("x0", "y0", "z0")), (("x0", "y0", "z0"), ("x1", "y1", "z1")))
C_PIECES = ((0, 2, 0), (3, 1, 1), (5, 1, 2), (2, 1, 0), (4, 1, 1), (6, 1, 2))


def all_pieces(groups, pieces):
    found = []
    for tile, count, turn in pieces:
        for at, (ring, _) in enumerate(groups):
            columns = pl.ds(at * HALF + tile * 128, count * 128)
            found.append((at, columns, ring[turn:] + ring[:turn]))
    return found


def subsets(bits):
    found = [tuple(bit for i, bit in enumerate(bits) if n >> i & 1) for n in range(1, 2 ** len(bits))]
    return sorted(found, key=lambda flips: -len(flips))


EVERY = slice(None)


class Sems:
    def __init__(self, sends, recvs):
        self.sends, self.recvs, self.count, self.pending = sends, recvs, 0, []

    def remote(self, source, target, landing, device):
        n = self.count
        self.count += 1
        copy = pltpu.make_async_remote_copy(
            src_ref=source,
            dst_ref=target,
            send_sem=self.sends.at[n],
            recv_sem=self.recvs.at[n],
            device_id=device,
            device_id_type=MESH,
        )
        copy.start()
        self.pending.append(copy)
        return pltpu.make_async_remote_copy(
            src_ref=source,
            dst_ref=landing,
            send_sem=self.sends.at[n],
            recv_sem=self.recvs.at[n],
            device_id=device,
            device_id_type=MESH,
        ).wait_recv


SEMS = 160


def kernel(
    len_ref, res_ref, ids_ref, rw_ref, vw_hbm, q_hbm, cache_hbm, wo_hbm, wg_hbm, wu_hbm, wd_hbm, out_ref,
    qv, cv, lat, mbuf, lbuf, rel, resq, wts, a2a, vw, wo, wg, wu, wd, resx, wx, hid, values, ab, rb, ss, ssr, tab, g,
    accg, accu, act, ah, rh, outs, fsend, frecv, loads, sends, recvs,
):
    role, dev = lax.axis_index("role"), lax.axis_index("dev")
    core, x, y, zl = dev % 2, (dev // 2) % 4, (dev // 8) % 4, dev // 32
    own = {
        "x1": x // 2, "x0": (x + x // 2) % 2, "y1": y // 2, "y0": (y + y // 2) % 2,
        "z1": role, "z0": (zl + role) % 2,
    }
    def across(*flips):
        at = {bit: 1 - own[bit] if bit in flips else own[bit] for bit in own}
        to_x = 2 * at["x1"] + (at["x1"] + at["x0"]) % 2
        to_y = 2 * at["y1"] + (at["y1"] + at["y0"]) % 2
        to_zl = (at["z1"] + at["z0"]) % 2
        return at["z1"], ((to_zl * 4 + to_y) * 4 + to_x) * 2 + core

    twin = (role, dev + 1 - 2 * core)
    sibling = 1 - core

    fetch = []

    def load(source, target):
        copy = pltpu.make_async_copy(source, target, loads.at[len(fetch)])
        copy.start()
        fetch.append(copy)
        return copy

    attention_loads = [(load(q_hbm.at[n], qv.at[n]), load(cache_hbm.at[n], cv.at[n])) for n in range(4)]
    vw_load = load(vw_hbm, vw.at[core])
    quarters = [pl.ds(q * Q, Q) for q in range(4)]
    wo_loads = [load(wo_hbm.at[:, quarters[q]], wo.at[q, core]) for q in range(4)]
    wg_load, wu_load = load(wg_hbm, wg.at[core]), load(wu_hbm, wu.at[core])
    wd_loads = [load(wd_hbm.at[:, quarters[q]], wd.at[q, core]) for q in range(4)]

    barrier = pltpu.get_barrier_semaphore()

    def greet(d, carry):
        pl.semaphore_signal(barrier, inc=1, device_id=(role, (dev + 2 * d) % HEADS), device_id_type=MESH)
        return carry

    lax.fori_loop(1, CHIPS, greet, 0)
    beyond = [across(*flips) for flips in subsets(("x1", "y1", "z1")) if "z1" in flips]
    for device in [twin] + beyond:
        pl.semaphore_signal(barrier, inc=1, device_id=device, device_id_type=MESH)

    for q in range(4):
        resq[q // 2, q % 2] = res_ref[:, q * Q:(q + 1) * Q].astype(F32)
    four_lanes = lax.broadcasted_iota(jnp.int32, (4, 128), 1)
    dense = jnp.zeros((4, 128), F32)
    for k in range(8):
        dense = dense + jnp.where(four_lanes == ids_ref[:, k:k + 1], rw_ref[:, k:k + 1], 0.0)
    wts[...] = dense

    slots = lax.broadcasted_iota(jnp.int32, (HEADS, LEN), 1)
    for pair in attention_loads:
        for copy in pair:
            copy.wait()
    scores = [jnp.dot(qv[n], cv[n], preferred_element_type=F32) * score_scale for n in range(4)]
    for n in range(4):
        live = jnp.where(slots < len_ref[n], scores[n], -jnp.inf)
        raised = jnp.exp(live - jnp.max(live, axis=1, keepdims=True))
        chances = (raised / jnp.sum(raised, axis=1, keepdims=True)).astype(BF)
        lat[n] = lax.dot_general(
            chances, cv[n, :KEY_VALUE_RANK, :], (((1,), (1,)), ((), ())), preferred_element_type=F32
        ).astype(BF)

    to = lax.broadcasted_iota(jnp.int32, (256, 256), 0)
    source = lax.broadcasted_iota(jnp.int32, (256, 256), 1)
    regroup = jnp.where(source == (to % 16) * 16 + to // 16, 1.0, 0.0).astype(BF)
    for group in range(4):
        heads = slice(16 * group, 16 * group + 16)
        pieces = [lat[n, heads, 128 * c:128 * c + 128] for c in range(4) for n in range(4)]
        moved = jnp.dot(regroup, jnp.concatenate(pieces, axis=0), preferred_element_type=F32)
        mbuf[8 * group:8 * group + 8] = moved.astype(BF).reshape(8, 2, 16, 128)

    pl.semaphore_wait(barrier, CHIPS + len(beyond))
    seat = ((own["z0"] * 2 + own["y1"]) * 2 + own["y0"]) * 4 + own["x1"] * 2 + own["x0"]

    def message(chip):
        return pltpu.make_async_remote_copy(
            src_ref=mbuf.at[chip], dst_ref=lbuf.at[seat], send_sem=a2a.at[0], recv_sem=a2a.at[1],
            device_id=(role, 2 * chip + core), device_id_type=MESH,
        )

    def post(d, carry):
        message((dev // 2 + d) % CHIPS).start()
        return carry

    lax.fori_loop(1, CHIPS, post, 0)
    lbuf[seat] = mbuf[dev // 2]

    sems = Sems(sends, recvs)
    x1, x0 = own["x1"], own["x0"]
    lines = (
        (across("x1", "x0"), 1 - x1, 1 - x0), (across("x1"), 1 - x1, x0), (across("x0"), x1, 1 - x0),
    )

    vw_wait = sems.remote(vw_hbm, vw.at[core], vw.at[sibling], twin)
    wo_waits = [
        sems.remote(wo_hbm.at[:, quarters[q]], wo.at[q, core], wo.at[q, sibling], twin) for q in range(4)
    ]

    arrivals = []
    for device, p1, p0 in lines:
        arrivals.append(sems.remote(resq.at[p1, p0], resx.at[x1, x0], resx.at[p1, p0], device))
        arrivals.append(sems.remote(wts, wx.at[x1, x0], wx.at[p1, p0], device))
    resx[x1, x0] = resq[x1, x0]
    wx[x1, x0] = wts[...]
    wg_wait = sems.remote(wg_hbm, wg.at[core], wg.at[sibling], twin)
    wu_wait = sems.remote(wu_hbm, wu.at[core], wu.at[sibling], twin)
    wd_waits = [
        sems.remote(wd_hbm.at[:, quarters[q]], wd.at[q, core], wd.at[q, sibling], twin) for q in range(4)
    ]

    spread = jnp.where(source == ((to % 64) // 4) * 16 + (to // 64) * 4 + to % 4, 1.0, 0.0).astype(BF)
    everyone = pltpu.make_async_remote_copy(
        src_ref=mbuf.at[pl.ds(0, CHIPS - 1)], dst_ref=lbuf.at[pl.ds(0, CHIPS - 1)],
        send_sem=a2a.at[0], recv_sem=a2a.at[1], device_id=twin, device_id_type=MESH,
    )
    everyone.wait_recv()
    for group in range(2):
        for head in range(2):
            rows = lbuf[16 * group:16 * group + 16, head].reshape(256, 128)
            moved = jnp.dot(spread, rows, preferred_element_type=F32).astype(BF)
            for c in range(4):
                rel[head, 64 * group:64 * group + 64, 128 * c:128 * c + 128] = moved[64 * c:64 * c + 64]

    def reduce_scatter(produce, buf, landing, dims, groups, pieces):
        found = all_pieces(groups, pieces)
        waits = [None] * len(found)

        def place(order, step, mine):
            indices = []
            for dim in dims:
                at = order.index(dim) if dim in order else len(order)
                here = own[dim] if mine else 1 - own[dim]
                indices.append(own[dim] if at < step else here if at == step else EVERY)
            return tuple(indices) + (EVERY,)

        def advance(n, step):
            _, columns, order = found[n]
            mine, other = place(order, step, True) + (columns,), place(order, step, False) + (columns,)
            if step < len(order):
                waits[n] = sems.remote(buf.at[other], landing.at[mine], landing.at[other], across(order[step]))

        def add(n, step):
            _, columns, order = found[n]
            waits[n]()
            mine, other = place(order, step, True) + (columns,), place(order, step, False) + (columns,)
            buf[mine] = buf[mine] + landing[other]

        for n, (_, columns, _) in enumerate(found):
            produce(buf, columns)
            advance(n, 0)
        rounds = len(groups[0][0])
        for step in range(1, rounds):
            for n in range(len(found)):
                add(n, step - 1)
                advance(n, step)
        result, last = [], []
        for at, (ring, direct) in enumerate(groups):
            columns = pl.ds(at * HALF, HALF)
            for n in range(len(found)):
                if found[n][0] == at:
                    add(n, rounds - 1)
            mine = tuple(own[dim] for dim in dims) + (EVERY, columns)
            others = []
            for flips in subsets(direct):
                other = tuple(1 - own[dim] if dim in flips else own[dim] for dim in dims) + (EVERY, columns)
                last.append(sems.remote(buf.at[other], landing.at[mine], landing.at[other], across(*flips)))
                others.append(other)
            result.append((columns, mine, others))
        for wait in last:
            wait()
        return result

    vw_load.wait()
    vw_wait()
    for head in range(2):
        values[:, HEAD * head:HEAD * head + HEAD] = jnp.dot(
            rel[head], vw[head], preferred_element_type=F32
        ).astype(BF)
    for copy in wo_loads:
        copy.wait()
    for wait in wo_waits:
        wait()

    def project(target, columns):
        width = columns.size
        weight = jnp.concatenate([wo[q, :, :, columns].reshape(2 * HEAD, width) for q in range(4)], axis=1)
        product = jnp.dot(values[...], weight, preferred_element_type=F32).astype(BF)
        for q in range(4):
            block = product[:, q * width:(q + 1) * width].reshape(2, 2, 2, 16, width)
            target[:, :, :, q // 2, q % 2, :, columns] = block

    summed = reduce_scatter(project, ab, rb, B_DIMS, B_GROUPS, B_PIECES)

    for wait in arrivals:
        wait()
    for j in range(4):
        hid[4 * j:4 * j + 4, :] = resx[j // 2, j % 2]
    block = tuple(own[dim] for dim in C_DIMS)
    squares = jnp.zeros((16, 1), F32)
    for columns, mine, others in summed:
        total = ab[mine].astype(F32)
        for other in others:
            total = total + rb[other].astype(F32)
        rounded = (hid[:, columns] + total).astype(BF)
        g[block + (EVERY, columns)] = rounded
        total = rounded.astype(F32)
        hid[:, columns] = total
        squares = squares + jnp.sum(total * total, axis=1, keepdims=True)

    direct_waits = []
    for at, (_, direct) in enumerate(C_GROUPS):
        columns = pl.ds(at * HALF, HALF)
        here = g.at[block + (EVERY, columns)]
        waits = []
        for flips in subsets(direct):
            other = tuple(1 - own[dim] if dim in flips else own[dim] for dim in C_DIMS)
            waits.append(sems.remote(here, here, g.at[other + (EVERY, columns)], across(*flips)))
        direct_waits.append(waits)

    ss[0] = jnp.broadcast_to(squares, (16, 128))
    square_waits = [
        sems.remote(ss.at[0], ssr.at[x1, x0], ssr.at[p1, p0], device) for device, p1, p0 in lines
    ]
    for wait in square_waits:
        wait()
    squares = ss[0]
    for _, p1, p0 in lines:
        squares = squares + ssr[p1, p0]
    weights = jnp.concatenate([wx[j // 2, j % 2] for j in range(4)], axis=0)
    lanes = lax.broadcasted_iota(jnp.int32, (16, 128), 1)
    scale = lax.rsqrt(squares * (1.0 / D) + 1e-06)
    table_at = (own["z1"], own["z0"], own["y1"], own["y0"])
    tab[table_at] = jnp.where(lanes == EXPERTS, scale, weights)

    def table_step(first, second, others):
        dims = ("z1", "z0", "y1", "y0")

        def at(flips):
            indices = []
            for dim in dims:
                if dim in (first, second):
                    indices.append(1 - own[dim] if dim in flips else own[dim])
                else:
                    indices.append(EVERY if others else own[dim])
            return tuple(indices)

        return [
            sems.remote(tab.at[at(())], tab.at[at(())], tab.at[at(flips)], across(*flips))
            for flips in subsets((first, second))
        ]

    found = all_pieces(C_GROUPS, C_PIECES)
    waits = [None] * len(found)

    def gather_place(n, step, mine):
        at, columns, order = found[n]
        indices = []
        for dim in C_DIMS:
            if dim not in order or order.index(dim) < step:
                indices.append(EVERY)
            elif order.index(dim) == step:
                indices.append(own[dim] if mine else 1 - own[dim])
            else:
                indices.append(own[dim])
        return tuple(indices) + (EVERY, columns)

    table_waits = table_step("y0", "z0", False)
    for step in range(3):
        for n in range(len(found)):
            if step:
                waits[n]()
            elif n < 2:
                for wait in direct_waits[n]:
                    wait()
            here = g.at[gather_place(n, step, True)]
            there = g.at[gather_place(n, step, False)]
            waits[n] = sems.remote(here, here, there, across(found[n][2][step]))
        if step < 2:
            for wait in table_waits:
                wait()
        if step == 0:
            table_waits = table_step("y1", "z1", True)

    wg_load.wait()
    wu_load.wait()
    wg_wait()
    wu_wait()
    for n, (_, columns, _) in enumerate(found):
        waits[n]()
        width = columns.size
        rows = jnp.concatenate(
            [g[:, :, :, :, q // 2, q % 2, :, columns].reshape(256, width) for q in range(4)], axis=1
        )
        for unit in range(2):
            for acc, weights in ((accg, wg), (accu, wu)):
                weight = jnp.concatenate([weights[unit, q, columns, :] for q in range(4)], axis=0)
                product = jnp.dot(rows, weight, preferred_element_type=F32)
                acc[unit] = acc[unit] + product if n else product
    expert = role * 8 + zl * 4 + y
    rows_lanes = lax.broadcasted_iota(jnp.int32, (256, 128), 1)
    table = tab[...].reshape(256, 128)
    route = jnp.sum(jnp.where(rows_lanes == expert, table, 0.0), axis=1, keepdims=True)
    scale = jnp.sum(jnp.where(rows_lanes == EXPERTS, table, 0.0), axis=1, keepdims=True)
    for unit in range(2):
        gate = accg[unit] * scale
        activated = jax.nn.silu(gate) * (accu[unit] * scale) * route
        act[:, FF * unit:FF * unit + FF] = activated.astype(BF)
    for copy in wd_loads:
        copy.wait()
    for wait in wd_waits:
        wait()

    def down(target, columns):
        width = columns.size
        weight = jnp.concatenate([wd[q, :, :, columns].reshape(2 * FF, width) for q in range(4)], axis=1)
        product = jnp.dot(act[...], weight, preferred_element_type=F32).astype(BF)
        for q in range(4):
            block = product[:, q * width:(q + 1) * width].reshape(2, 2, 2, 2, 16, width)
            target[:, :, :, :, q // 2, q % 2, :, columns] = block

    summed = reduce_scatter(down, ah, rh, C_DIMS, C_GROUPS, C_PIECES)
    for columns, mine, others in summed:
        total = hid[:, columns] + ah[mine].astype(F32)
        for other in others:
            total = total + rh[other].astype(F32)
        outs[:, columns] = total

    for j in range(4):
        fsend[j // 2, j % 2] = outs[4 * j:4 * j + 4, :]
    waits = [
        sems.remote(fsend.at[p1, p0], frecv.at[x1, x0], frecv.at[p1, p0], device)
        for device, p1, p0 in lines
    ]
    frecv[x1, x0] = fsend[x1, x0]
    for wait in waits:
        wait()
    for j in range(4):
        out_ref[:, j * Q:(j + 1) * Q] = frecv[j // 2, j % 2].astype(BF)
    assert sems.count <= SEMS
    everyone.wait_send()
    for copy in sems.pending:
        copy.wait_send()


def layer(*operands):
    vmem = pl.BlockSpec(memory_space=pltpu.VMEM)
    hbm = pl.BlockSpec(memory_space=pl.ANY)
    b_shape, c_shape = (2,) * 5 + (16, Q), (2,) * 6 + (16, Q)
    return pl.pallas_call(
        kernel,
        out_shape=jax.ShapeDtypeStruct((4, D), BF),
        in_specs=[pl.BlockSpec(memory_space=pltpu.SMEM)] + [vmem] * 3 + [hbm] * 7,
        out_specs=vmem,
        scratch_shapes=[
            pltpu.VMEM((4, HEADS, LATENT), BF),
            pltpu.VMEM((4, LATENT, LEN), BF),
            pltpu.VMEM((4, HEADS, KEY_VALUE_RANK), BF),
            pltpu.VMEM((CHIPS, 2, 16, 128), BF),
            pltpu.VMEM((CHIPS, 2, 16, 128), BF),
            pltpu.VMEM((2, 128, KEY_VALUE_RANK), BF),
            pltpu.VMEM((2, 2, 4, Q), F32),
            pltpu.VMEM((4, 128), F32),
            pltpu.SemaphoreType.DMA((2,)),
            pltpu.VMEM((2, KEY_VALUE_RANK, HEAD), BF),
            pltpu.VMEM((4, 2, HEAD, Q), BF),
            pltpu.VMEM((2, 4, Q, FF), BF),
            pltpu.VMEM((2, 4, Q, FF), BF),
            pltpu.VMEM((4, 2, FF, Q), BF),
            pltpu.VMEM((2, 2, 4, Q), F32),
            pltpu.VMEM((2, 2, 4, 128), F32),
            pltpu.VMEM((16, Q), F32),
            pltpu.VMEM((128, 2 * HEAD), BF),
            pltpu.VMEM(b_shape, BF),
            pltpu.VMEM(b_shape, BF),
            pltpu.VMEM((1, 16, 128), F32),
            pltpu.VMEM((2, 2, 16, 128), F32),
            pltpu.VMEM((2,) * 4 + (16, 128), F32),
            pltpu.VMEM(c_shape, BF),
            pltpu.VMEM((2, 256, FF), F32),
            pltpu.VMEM((2, 256, FF), F32),
            pltpu.VMEM((256, 2 * FF), BF),
            pltpu.VMEM(c_shape, BF),
            pltpu.VMEM(c_shape, BF),
            pltpu.VMEM((16, Q), F32),
            pltpu.VMEM((2, 2, 4, Q), F32),
            pltpu.VMEM((2, 2, 4, Q), F32),
            pltpu.SemaphoreType.DMA((19,)),
            pltpu.SemaphoreType.DMA((SEMS,)),
            pltpu.SemaphoreType.DMA((SEMS,)),
        ],
        compiler_params=pltpu.CompilerParams(
            collective_id=0, has_side_effects=True, vmem_limit_bytes=58 * 2**20
        ),
    )(*operands)


def local(
    queries, latent_cache, cache_lengths, residual, expert_ids, route_weights,
    value_weight, w_out, w_gate, w_up, w_down,
):
    return layer(
        cache_lengths, residual, expert_ids, route_weights, value_weight[0], queries, latent_cache.transpose(0, 2, 1), w_out,
        w_gate.reshape(4, Q, FF), w_up.reshape(4, Q, FF), w_down[0],
    )


def solution(mesh):
    return jax.shard_map(
        local,
        mesh=mesh,
        in_specs=(
            P(("role", "dev"), None, None),
            P(("role", "dev"), None, None),
            P(("role", "dev")),
            P(("role", "dev"), None),
            P(("role", "dev"), None),
            P(("role", "dev"), None),
            P("dev", None, None),
            P("dev", None),
            P(("role", "dev"), None, None),
            P(("role", "dev"), None, None),
            P(("role", "dev"), None, None),
        ),
        out_specs=P(("role", "dev"), None),
        check_vma=False,
    )
```

```python
import math

import jax
import jax.numpy as jnp
from jax import lax
from jax.experimental import pallas as pl
from jax.experimental.pallas import tpu as pltpu
from jax.sharding import PartitionSpec as P

KEY_VALUE_RANK = 512
HEADS = 64
CHIPS = HEADS // 2
LEN = 512
LATENT = 576
EXPERTS = 16
MESH = pl.DeviceIdType.MESH
D = 7168
Q = D // 4
FF = 256
HEAD = 128
BF = jnp.bfloat16
F32 = jnp.float32
score_scale = 1.0 / math.sqrt(192.0)


B_DIMS = ("z0", "y1", "y0", "x1", "x0")
C_DIMS = ("z1",) + B_DIMS
HALF = Q // 2
B_GROUPS = ((("x1", "y1"), ("x0", "y0", "z0")), (("x0", "y0"), ("x1", "y1", "z0")))
B_PIECES = (
    (0, 2, 0, None), (3, 2, 1, None), (2, 1, 0, None), (5, 1, 1, None), (6, 1, 0, 0), (6, 1, 1, 1),
)
C_GROUPS = ((("x1", "y1", "z1"), ("x0", "y0", "z0")), (("x0", "y0", "z0"), ("x1", "y1", "z1")))
C_PIECES = (
    (0, 1, 0, None), (3, 1, 1, None), (5, 1, 2, None), (1, 1, 0, None), (4, 1, 1, None), (6, 1, 2, None),
    (2, 1, 0, 0), (2, 1, 1, 1),
)


def all_pieces(groups, pieces):
    found = []
    for tile, count, turn, half in pieces:
        for at, (ring, direct) in enumerate(groups):
            columns = pl.ds(at * HALF + tile * 128, count * 128)
            found.append((at, columns, ring[turn:] + ring[:turn], {} if half is None else {direct[0]: half}))
    return found


def subsets(bits):
    found = [tuple(bit for i, bit in enumerate(bits) if n >> i & 1) for n in range(1, 2 ** len(bits))]
    return sorted(found, key=lambda flips: -len(flips))


EVERY = slice(None)


class Sems:
    def __init__(self, sends, recvs):
        self.sends, self.recvs, self.count, self.pending = sends, recvs, 0, []

    def remote(self, source, target, landing, device):
        n = self.count
        self.count += 1
        copy = pltpu.make_async_remote_copy(
            src_ref=source,
            dst_ref=target,
            send_sem=self.sends.at[n],
            recv_sem=self.recvs.at[n],
            device_id=device,
            device_id_type=MESH,
        )
        copy.start()
        self.pending.append(copy)
        return pltpu.make_async_remote_copy(
            src_ref=source,
            dst_ref=landing,
            send_sem=self.sends.at[n],
            recv_sem=self.recvs.at[n],
            device_id=device,
            device_id_type=MESH,
        ).wait_recv


SEMS = 192


def kernel(
    len_ref, res_ref, ids_ref, rw_ref, vw_hbm, q_hbm, cache_hbm, wo_hbm, wg_hbm, wu_hbm, wd_hbm, out_ref,
    qv, cv, lat, mbuf, lbuf, rel, resq, wts, a2a, vw, wo, wg, wu, wd, resx, wx, hid, values, ab, rb, ss, ssr, tab, g,
    accg, accu, act, ah, rh, outs, fsend, frecv, loads, sends, recvs,
):
    role, dev = lax.axis_index("role"), lax.axis_index("dev")
    core, x, y, zl = dev % 2, (dev // 2) % 4, (dev // 8) % 4, dev // 32
    own = {
        "x1": x // 2, "x0": (x + x // 2) % 2, "y1": y // 2, "y0": (y + y // 2) % 2,
        "z1": role, "z0": (zl + role) % 2,
    }
    def across(*flips):
        at = {bit: 1 - own[bit] if bit in flips else own[bit] for bit in own}
        to_x = 2 * at["x1"] + (at["x1"] + at["x0"]) % 2
        to_y = 2 * at["y1"] + (at["y1"] + at["y0"]) % 2
        to_zl = (at["z1"] + at["z0"]) % 2
        return at["z1"], ((to_zl * 4 + to_y) * 4 + to_x) * 2 + core

    twin = (role, dev + 1 - 2 * core)
    sibling = 1 - core

    fetch = []

    def load(source, target):
        copy = pltpu.make_async_copy(source, target, loads.at[len(fetch)])
        copy.start()
        fetch.append(copy)
        return copy

    attention_loads = [(load(q_hbm.at[n], qv.at[n]), load(cache_hbm.at[n], cv.at[n])) for n in range(4)]
    vw_load = load(vw_hbm, vw.at[core])
    quarters = [pl.ds(q * Q, Q) for q in range(4)]
    wo_loads = [load(wo_hbm.at[:, quarters[q]], wo.at[q, core]) for q in range(4)]
    wg_load, wu_load = load(wg_hbm, wg.at[core]), load(wu_hbm, wu.at[core])
    wd_loads = [load(wd_hbm.at[:, quarters[q]], wd.at[q, core]) for q in range(4)]

    barrier = pltpu.get_barrier_semaphore()

    def greet(d, carry):
        pl.semaphore_signal(barrier, inc=1, device_id=(role, (dev + 2 * d) % HEADS), device_id_type=MESH)
        return carry

    lax.fori_loop(1, CHIPS, greet, 0)
    beyond = [across(*flips) for flips in subsets(("x1", "y1", "z1")) if "z1" in flips]
    for device in [twin] + beyond:
        pl.semaphore_signal(barrier, inc=1, device_id=device, device_id_type=MESH)

    for q in range(4):
        resq[q // 2, q % 2] = res_ref[:, q * Q:(q + 1) * Q].astype(F32)
    four_lanes = lax.broadcasted_iota(jnp.int32, (4, 128), 1)
    dense = jnp.zeros((4, 128), F32)
    for k in range(8):
        dense = dense + jnp.where(four_lanes == ids_ref[:, k:k + 1], rw_ref[:, k:k + 1], 0.0)
    wts[...] = dense

    slots = lax.broadcasted_iota(jnp.int32, (HEADS, LEN), 1)
    for pair in attention_loads:
        for copy in pair:
            copy.wait()
    scores = [jnp.dot(qv[n], cv[n], preferred_element_type=F32) * score_scale for n in range(4)]
    for n in range(4):
        live = jnp.where(slots < len_ref[n], scores[n], -jnp.inf)
        raised = jnp.exp(live - jnp.max(live, axis=1, keepdims=True))
        chances = (raised / jnp.sum(raised, axis=1, keepdims=True)).astype(BF)
        lat[n] = lax.dot_general(
            chances, cv[n, :KEY_VALUE_RANK, :], (((1,), (1,)), ((), ())), preferred_element_type=F32
        ).astype(BF)

    to = lax.broadcasted_iota(jnp.int32, (256, 256), 0)
    source = lax.broadcasted_iota(jnp.int32, (256, 256), 1)
    regroup = jnp.where(source == (to % 16) * 16 + to // 16, 1.0, 0.0).astype(BF)
    for group in range(4):
        heads = slice(16 * group, 16 * group + 16)
        pieces = [lat[n, heads, 128 * c:128 * c + 128] for c in range(4) for n in range(4)]
        moved = jnp.dot(regroup, jnp.concatenate(pieces, axis=0), preferred_element_type=F32)
        mbuf[8 * group:8 * group + 8] = moved.astype(BF).reshape(8, 2, 16, 128)

    pl.semaphore_wait(barrier, CHIPS + len(beyond))
    seat = ((own["z0"] * 2 + own["y1"]) * 2 + own["y0"]) * 4 + own["x1"] * 2 + own["x0"]

    def message(chip):
        return pltpu.make_async_remote_copy(
            src_ref=mbuf.at[chip], dst_ref=lbuf.at[seat], send_sem=a2a.at[0], recv_sem=a2a.at[1],
            device_id=(role, 2 * chip + core), device_id_type=MESH,
        )

    def post(d, carry):
        message((dev // 2 + d) % CHIPS).start()
        return carry

    lax.fori_loop(1, CHIPS, post, 0)
    lbuf[seat] = mbuf[dev // 2]

    sems = Sems(sends, recvs)
    x1, x0 = own["x1"], own["x0"]
    lines = (
        (across("x1", "x0"), 1 - x1, 1 - x0), (across("x1"), 1 - x1, x0), (across("x0"), x1, 1 - x0),
    )

    vw_wait = sems.remote(vw_hbm, vw.at[core], vw.at[sibling], twin)
    wo_waits = [
        sems.remote(wo_hbm.at[:, quarters[q]], wo.at[q, core], wo.at[q, sibling], twin) for q in range(4)
    ]

    arrivals = []
    for device, p1, p0 in lines:
        arrivals.append(sems.remote(resq.at[p1, p0], resx.at[x1, x0], resx.at[p1, p0], device))
        arrivals.append(sems.remote(wts, wx.at[x1, x0], wx.at[p1, p0], device))
    resx[x1, x0] = resq[x1, x0]
    wx[x1, x0] = wts[...]
    wg_wait = sems.remote(wg_hbm, wg.at[core], wg.at[sibling], twin)
    wu_wait = sems.remote(wu_hbm, wu.at[core], wu.at[sibling], twin)
    wd_waits = [
        sems.remote(wd_hbm.at[:, quarters[q]], wd.at[q, core], wd.at[q, sibling], twin) for q in range(4)
    ]

    spread = jnp.where(source == ((to % 64) // 4) * 16 + (to // 64) * 4 + to % 4, 1.0, 0.0).astype(BF)
    everyone = pltpu.make_async_remote_copy(
        src_ref=mbuf.at[pl.ds(0, CHIPS - 1)], dst_ref=lbuf.at[pl.ds(0, CHIPS - 1)],
        send_sem=a2a.at[0], recv_sem=a2a.at[1], device_id=twin, device_id_type=MESH,
    )
    everyone.wait_recv()
    for group in range(2):
        for head in range(2):
            rows = lbuf[16 * group:16 * group + 16, head].reshape(256, 128)
            moved = jnp.dot(spread, rows, preferred_element_type=F32).astype(BF)
            for c in range(4):
                rel[head, 64 * group:64 * group + 64, 128 * c:128 * c + 128] = moved[64 * c:64 * c + 64]

    def reduce_scatter(produce, buf, landing, dims, groups, pieces):
        found = all_pieces(groups, pieces)
        waits = [None] * len(found)

        def place(n, step, mine):
            _, columns, order, confined = found[n]
            indices = []
            for dim in dims:
                if dim in confined:
                    indices.append(confined[dim])
                    continue
                at = order.index(dim) if dim in order else len(order)
                here = own[dim] if mine else 1 - own[dim]
                indices.append(own[dim] if at < step else here if at == step else EVERY)
            return tuple(indices) + (EVERY, columns)

        def advance(n, step):
            order = found[n][2]
            mine, other = place(n, step, True), place(n, step, False)
            if step < len(order):
                waits[n] = sems.remote(buf.at[other], landing.at[mine], landing.at[other], across(order[step]))

        def add(n, step):
            waits[n]()
            mine, other = place(n, step, True), place(n, step, False)
            buf[mine] = buf[mine] + landing[other]

        for n, (_, columns, _, confined) in enumerate(found):
            if 1 not in confined.values():
                produce(buf, columns)
            advance(n, 0)
        rounds = len(groups[0][0])
        for step in range(1, rounds):
            for n in range(len(found)):
                add(n, step - 1)
                advance(n, step)
        result, last = [], []
        for at, (ring, direct) in enumerate(groups):
            columns = pl.ds(at * HALF, HALF)
            for n in range(len(found)):
                if found[n][0] == at:
                    add(n, rounds - 1)
            mine = tuple(own[dim] for dim in dims) + (EVERY, columns)
            others = []
            for flips in subsets(direct):
                other = tuple(1 - own[dim] if dim in flips else own[dim] for dim in dims) + (EVERY, columns)
                last.append(sems.remote(buf.at[other], landing.at[mine], landing.at[other], across(*flips)))
                others.append(other)
            result.append((columns, mine, others))
        for wait in last:
            wait()
        return result

    vw_load.wait()
    vw_wait()
    for head in range(2):
        values[:, HEAD * head:HEAD * head + HEAD] = jnp.dot(
            rel[head], vw[head], preferred_element_type=F32
        ).astype(BF)
    for copy in wo_loads:
        copy.wait()
    for wait in wo_waits:
        wait()

    def project(target, columns):
        width = columns.size
        weight = jnp.concatenate([wo[q, :, :, columns].reshape(2 * HEAD, width) for q in range(4)], axis=1)
        product = jnp.dot(values[...], weight, preferred_element_type=F32).astype(BF)
        for q in range(4):
            block = product[:, q * width:(q + 1) * width].reshape(2, 2, 2, 16, width)
            target[:, :, :, q // 2, q % 2, :, columns] = block

    summed = reduce_scatter(project, ab, rb, B_DIMS, B_GROUPS, B_PIECES)

    for wait in arrivals:
        wait()
    for j in range(4):
        hid[4 * j:4 * j + 4, :] = resx[j // 2, j % 2]
    block = tuple(own[dim] for dim in C_DIMS)
    squares = jnp.zeros((16, 1), F32)
    for columns, mine, others in summed:
        total = ab[mine].astype(F32)
        for other in others:
            total = total + rb[other].astype(F32)
        rounded = (hid[:, columns] + total).astype(BF)
        g[block + (EVERY, columns)] = rounded
        total = rounded.astype(F32)
        hid[:, columns] = total
        squares = squares + jnp.sum(total * total, axis=1, keepdims=True)

    direct_waits = []
    for at, (_, direct) in enumerate(C_GROUPS):
        columns = pl.ds(at * HALF, HALF)
        here = g.at[block + (EVERY, columns)]
        waits = []
        for flips in subsets(direct):
            other = tuple(1 - own[dim] if dim in flips else own[dim] for dim in C_DIMS)
            waits.append(sems.remote(here, here, g.at[other + (EVERY, columns)], across(*flips)))
        direct_waits.append(waits)

    ss[0] = jnp.broadcast_to(squares, (16, 128))
    square_waits = [
        sems.remote(ss.at[0], ssr.at[x1, x0], ssr.at[p1, p0], device) for device, p1, p0 in lines
    ]
    for wait in square_waits:
        wait()
    squares = ss[0]
    for _, p1, p0 in lines:
        squares = squares + ssr[p1, p0]
    weights = jnp.concatenate([wx[j // 2, j % 2] for j in range(4)], axis=0)
    lanes = lax.broadcasted_iota(jnp.int32, (16, 128), 1)
    scale = lax.rsqrt(squares * (1.0 / D) + 1e-06)
    table_at = (own["z1"], own["z0"], own["y1"], own["y0"])
    tab[table_at] = jnp.where(lanes == EXPERTS, scale, weights)

    def table_step(first, second, others):
        dims = ("z1", "z0", "y1", "y0")

        def at(flips):
            indices = []
            for dim in dims:
                if dim in (first, second):
                    indices.append(1 - own[dim] if dim in flips else own[dim])
                else:
                    indices.append(EVERY if others else own[dim])
            return tuple(indices)

        return [
            sems.remote(tab.at[at(())], tab.at[at(())], tab.at[at(flips)], across(*flips))
            for flips in subsets((first, second))
        ]

    found = all_pieces(C_GROUPS, C_PIECES)
    waits = [None] * len(found)

    def gather_place(n, step, mine):
        _, columns, order, confined = found[n]
        indices = []
        for dim in C_DIMS:
            if dim in confined:
                indices.append(confined[dim])
            elif dim not in order or order.index(dim) < step:
                indices.append(EVERY)
            elif order.index(dim) == step:
                indices.append(own[dim] if mine else 1 - own[dim])
            else:
                indices.append(own[dim])
        return tuple(indices) + (EVERY, columns)

    table_waits = table_step("y0", "z0", False)
    for step in range(3):
        for n in range(len(found)):
            if step:
                waits[n]()
            elif n < 2:
                for wait in direct_waits[n]:
                    wait()
            here = g.at[gather_place(n, step, True)]
            there = g.at[gather_place(n, step, False)]
            waits[n] = sems.remote(here, here, there, across(found[n][2][step]))
        if step < 2:
            for wait in table_waits:
                wait()
        if step == 0:
            table_waits = table_step("y1", "z1", True)

    wg_load.wait()
    wu_load.wait()
    wg_wait()
    wu_wait()
    batch, first = [], True
    for n, (_, columns, _, confined) in enumerate(found):
        waits[n]()
        if 0 not in confined.values():
            batch.append(columns)
        if n % 6 < 5 and n < len(found) - 1:
            continue
        rows = jnp.concatenate(
            [
                g[:, :, :, :, q // 2, q % 2, :, tile].reshape(256, tile.size)
                for tile in batch for q in range(4)
            ],
            axis=1,
        )
        for unit in range(2):
            for acc, weights in ((accg, wg), (accu, wu)):
                weight = jnp.concatenate(
                    [weights[unit, q, tile, :] for tile in batch for q in range(4)], axis=0
                )
                product = jnp.dot(rows, weight, preferred_element_type=F32)
                acc[unit] = product if first else acc[unit] + product
        batch, first = [], False
    expert = role * 8 + zl * 4 + y
    rows_lanes = lax.broadcasted_iota(jnp.int32, (256, 128), 1)
    table = tab[...].reshape(256, 128)
    route = jnp.sum(jnp.where(rows_lanes == expert, table, 0.0), axis=1, keepdims=True)
    scale = jnp.sum(jnp.where(rows_lanes == EXPERTS, table, 0.0), axis=1, keepdims=True)
    for unit in range(2):
        gate = accg[unit] * scale
        activated = jax.nn.silu(gate) * (accu[unit] * scale) * route
        act[:, FF * unit:FF * unit + FF] = activated.astype(BF)
    for copy in wd_loads:
        copy.wait()
    for wait in wd_waits:
        wait()

    def down(target, columns):
        width = columns.size
        weight = jnp.concatenate([wd[q, :, :, columns].reshape(2 * FF, width) for q in range(4)], axis=1)
        product = jnp.dot(act[...], weight, preferred_element_type=F32).astype(BF)
        for q in range(4):
            block = product[:, q * width:(q + 1) * width].reshape(2, 2, 2, 2, 16, width)
            target[:, :, :, :, q // 2, q % 2, :, columns] = block

    summed = reduce_scatter(down, ah, rh, C_DIMS, C_GROUPS, C_PIECES)
    for columns, mine, others in summed:
        total = hid[:, columns] + ah[mine].astype(F32)
        for other in others:
            total = total + rh[other].astype(F32)
        outs[:, columns] = total

    for j in range(4):
        fsend[j // 2, j % 2] = outs[4 * j:4 * j + 4, :]
    waits = [
        sems.remote(fsend.at[p1, p0], frecv.at[x1, x0], frecv.at[p1, p0], device)
        for device, p1, p0 in lines
    ]
    frecv[x1, x0] = fsend[x1, x0]
    for wait in waits:
        wait()
    for j in range(4):
        out_ref[:, j * Q:(j + 1) * Q] = frecv[j // 2, j % 2].astype(BF)
    assert sems.count <= SEMS
    everyone.wait_send()
    for copy in sems.pending:
        copy.wait_send()


def layer(*operands):
    vmem = pl.BlockSpec(memory_space=pltpu.VMEM)
    hbm = pl.BlockSpec(memory_space=pl.ANY)
    b_shape, c_shape = (2,) * 5 + (16, Q), (2,) * 6 + (16, Q)
    return pl.pallas_call(
        kernel,
        out_shape=jax.ShapeDtypeStruct((4, D), BF),
        in_specs=[pl.BlockSpec(memory_space=pltpu.SMEM)] + [vmem] * 3 + [hbm] * 7,
        out_specs=vmem,
        scratch_shapes=[
            pltpu.VMEM((4, HEADS, LATENT), BF),
            pltpu.VMEM((4, LATENT, LEN), BF),
            pltpu.VMEM((4, HEADS, KEY_VALUE_RANK), BF),
            pltpu.VMEM((CHIPS, 2, 16, 128), BF),
            pltpu.VMEM((CHIPS, 2, 16, 128), BF),
            pltpu.VMEM((2, 128, KEY_VALUE_RANK), BF),
            pltpu.VMEM((2, 2, 4, Q), F32),
            pltpu.VMEM((4, 128), F32),
            pltpu.SemaphoreType.DMA((2,)),
            pltpu.VMEM((2, KEY_VALUE_RANK, HEAD), BF),
            pltpu.VMEM((4, 2, HEAD, Q), BF),
            pltpu.VMEM((2, 4, Q, FF), BF),
            pltpu.VMEM((2, 4, Q, FF), BF),
            pltpu.VMEM((4, 2, FF, Q), BF),
            pltpu.VMEM((2, 2, 4, Q), F32),
            pltpu.VMEM((2, 2, 4, 128), F32),
            pltpu.VMEM((16, Q), F32),
            pltpu.VMEM((128, 2 * HEAD), BF),
            pltpu.VMEM(b_shape, BF),
            pltpu.VMEM(b_shape, BF),
            pltpu.VMEM((1, 16, 128), F32),
            pltpu.VMEM((2, 2, 16, 128), F32),
            pltpu.VMEM((2,) * 4 + (16, 128), F32),
            pltpu.VMEM(c_shape, BF),
            pltpu.VMEM((2, 256, FF), F32),
            pltpu.VMEM((2, 256, FF), F32),
            pltpu.VMEM((256, 2 * FF), BF),
            pltpu.VMEM(c_shape, BF),
            pltpu.VMEM(c_shape, BF),
            pltpu.VMEM((16, Q), F32),
            pltpu.VMEM((2, 2, 4, Q), F32),
            pltpu.VMEM((2, 2, 4, Q), F32),
            pltpu.SemaphoreType.DMA((19,)),
            pltpu.SemaphoreType.DMA((SEMS,)),
            pltpu.SemaphoreType.DMA((SEMS,)),
        ],
        compiler_params=pltpu.CompilerParams(
            collective_id=0, has_side_effects=True, vmem_limit_bytes=58 * 2**20
        ),
    )(*operands)


def local(
    queries, latent_cache, cache_lengths, residual, expert_ids, route_weights,
    value_weight, w_out, w_gate, w_up, w_down,
):
    return layer(
        cache_lengths, residual, expert_ids, route_weights, value_weight[0], queries, latent_cache.transpose(0, 2, 1), w_out,
        w_gate.reshape(4, Q, FF), w_up.reshape(4, Q, FF), w_down[0],
    )


def solution(mesh):
    return jax.shard_map(
        local,
        mesh=mesh,
        in_specs=(
            P(("role", "dev"), None, None),
            P(("role", "dev"), None, None),
            P(("role", "dev")),
            P(("role", "dev"), None),
            P(("role", "dev"), None),
            P(("role", "dev"), None),
            P("dev", None, None),
            P("dev", None),
            P(("role", "dev"), None, None),
            P(("role", "dev"), None, None),
            P(("role", "dev"), None, None),
        ),
        out_specs=P(("role", "dev"), None),
        check_vma=False,
    )
```

```python
import math

import jax
import jax.numpy as jnp
from jax import lax
from jax.experimental import pallas as pl
from jax.experimental.pallas import tpu as pltpu
from jax.sharding import PartitionSpec as P

KEY_VALUE_RANK = 512
HEADS = 64
CHIPS = HEADS // 2
LEN = 512
LATENT = 576
EXPERTS = 16
MESH = pl.DeviceIdType.MESH
D = 7168
Q = D // 4
FF = 256
HEAD = 128
BF = jnp.bfloat16
F32 = jnp.float32
score_scale = 1.0 / math.sqrt(192.0)


B_DIMS = ("z0", "y1", "y0", "x1", "x0")
C_DIMS = ("z1",) + B_DIMS
HALF = Q // 2
B_GROUPS = ((("x1", "y1"), ("x0", "y0", "z0")), (("x0", "y0"), ("x1", "y1", "z0")))
B_PIECES = (
    (0, 2, 0, None), (3, 2, 1, None), (2, 1, 0, None), (5, 1, 1, None), (6, 1, 0, 0), (6, 1, 1, 1),
)
C_GROUPS = ((("x1", "y1", "z1"), ("x0", "y0", "z0")), (("x0", "y0", "z0"), ("x1", "y1", "z1")))
C_PIECES = (
    (0, 1, 0, None), (3, 1, 1, None), (5, 1, 2, None), (1, 1, 0, None), (4, 1, 1, None), (6, 1, 2, None),
    (2, 1, 0, 0), (2, 1, 1, 1),
)


def all_pieces(groups, pieces):
    found = []
    for tile, count, turn, half in pieces:
        for at, (ring, direct) in enumerate(groups):
            columns = pl.ds(at * HALF + tile * 128, count * 128)
            found.append((at, columns, ring[turn:] + ring[:turn], {} if half is None else {direct[0]: half}))
    return found


def subsets(bits):
    found = [tuple(bit for i, bit in enumerate(bits) if n >> i & 1) for n in range(1, 2 ** len(bits))]
    return sorted(found, key=lambda flips: -len(flips))


EVERY = slice(None)


class Sems:
    def __init__(self, sends, recvs):
        self.sends, self.recvs, self.count, self.pending = sends, recvs, 0, []

    def drain(self, count):
        for copy in self.pending[:count]:
            copy.wait_send()
        self.pending = self.pending[count:]

    def remote(self, source, target, landing, device):
        n = self.count
        self.count += 1
        copy = pltpu.make_async_remote_copy(
            src_ref=source,
            dst_ref=target,
            send_sem=self.sends.at[n],
            recv_sem=self.recvs.at[n],
            device_id=device,
            device_id_type=MESH,
        )
        copy.start()
        self.pending.append(copy)
        return pltpu.make_async_remote_copy(
            src_ref=source,
            dst_ref=landing,
            send_sem=self.sends.at[n],
            recv_sem=self.recvs.at[n],
            device_id=device,
            device_id_type=MESH,
        ).wait_recv


SEMS = 192


def kernel(
    len_ref, res_ref, ids_ref, rw_ref, vw_hbm, q_hbm, cache_hbm, wo_hbm, wg_hbm, wu_hbm, wd_hbm, out_ref,
    qv, cv, lat, mbuf, lbuf, rel, resq, wts, a2a, vw, wo, wg, wu, wd, resx, wx, hid, values, ab, rb, ss, ssr, tab, g,
    accg, accu, act, ah, rh, outs, fsend, frecv, loads, sends, recvs,
):
    role, dev = lax.axis_index("role"), lax.axis_index("dev")
    core, x, y, zl = dev % 2, (dev // 2) % 4, (dev // 8) % 4, dev // 32
    own = {
        "x1": x // 2, "x0": (x + x // 2) % 2, "y1": y // 2, "y0": (y + y // 2) % 2,
        "z1": role, "z0": (zl + role) % 2,
    }
    def across(*flips):
        at = {bit: 1 - own[bit] if bit in flips else own[bit] for bit in own}
        to_x = 2 * at["x1"] + (at["x1"] + at["x0"]) % 2
        to_y = 2 * at["y1"] + (at["y1"] + at["y0"]) % 2
        to_zl = (at["z1"] + at["z0"]) % 2
        return at["z1"], ((to_zl * 4 + to_y) * 4 + to_x) * 2 + core

    twin = (role, dev + 1 - 2 * core)
    sibling = 1 - core

    fetch = []

    def load(source, target):
        copy = pltpu.make_async_copy(source, target, loads.at[len(fetch)])
        copy.start()
        fetch.append(copy)
        return copy

    attention_loads = [(load(q_hbm.at[n], qv.at[n]), load(cache_hbm.at[n], cv.at[n])) for n in range(4)]
    vw_load = load(vw_hbm, vw.at[core])
    quarters = [pl.ds(q * Q, Q) for q in range(4)]
    wo_loads = [load(wo_hbm.at[:, quarters[q]], wo.at[q, core]) for q in range(4)]
    wg_load, wu_load = load(wg_hbm, wg.at[core]), load(wu_hbm, wu.at[core])
    wd_loads = [load(wd_hbm.at[:, quarters[q]], wd.at[q, core]) for q in range(4)]

    sems = Sems(sends, recvs)
    barrier = pltpu.get_barrier_semaphore()

    def greet(d, carry):
        pl.semaphore_signal(barrier, inc=1, device_id=(role, (dev + 2 * d) % HEADS), device_id_type=MESH)
        return carry

    lax.fori_loop(1, CHIPS, greet, 0)
    beyond = [across(*flips) for flips in subsets(("x1", "y1", "z1")) if "z1" in flips]
    for device in [twin] + beyond:
        pl.semaphore_signal(barrier, inc=1, device_id=device, device_id_type=MESH)

    for q in range(4):
        resq[q // 2, q % 2] = res_ref[:, q * Q:(q + 1) * Q].astype(F32)
    four_lanes = lax.broadcasted_iota(jnp.int32, (4, 128), 1)
    dense = jnp.zeros((4, 128), F32)
    for k in range(8):
        dense = dense + jnp.where(four_lanes == ids_ref[:, k:k + 1], rw_ref[:, k:k + 1], 0.0)
    wts[...] = dense

    slots = lax.broadcasted_iota(jnp.int32, (HEADS, LEN), 1)
    for pair in attention_loads:
        for copy in pair:
            copy.wait()
    def attend(requests):
        scores = [jnp.dot(qv[n], cv[n], preferred_element_type=F32) * score_scale for n in requests]
        for n, score in zip(requests, scores):
            live = jnp.where(slots < len_ref[n], score, -jnp.inf)
            raised = jnp.exp(live - jnp.max(live, axis=1, keepdims=True))
            chances = (raised / jnp.sum(raised, axis=1, keepdims=True)).astype(BF)
            lat[n] = lax.dot_general(
                chances, cv[n, :KEY_VALUE_RANK, :], (((1,), (1,)), ((), ())), preferred_element_type=F32
            ).astype(BF)

    attend((0, 1))

    pl.semaphore_wait(barrier, CHIPS + len(beyond))
    vw_wait = sems.remote(vw_hbm, vw.at[core], vw.at[sibling], twin)
    wo_waits = [
        sems.remote(wo_hbm.at[:, quarters[q]], wo.at[q, core], wo.at[q, sibling], twin) for q in range(4)
    ]

    attend((2, 3))

    to = lax.broadcasted_iota(jnp.int32, (256, 256), 0)
    source = lax.broadcasted_iota(jnp.int32, (256, 256), 1)
    regroup = jnp.where(source == (to % 16) * 16 + to // 16, 1.0, 0.0).astype(BF)
    for group in range(4):
        heads = slice(16 * group, 16 * group + 16)
        pieces = [lat[n, heads, 128 * c:128 * c + 128] for c in range(4) for n in range(4)]
        moved = jnp.dot(regroup, jnp.concatenate(pieces, axis=0), preferred_element_type=F32)
        mbuf[8 * group:8 * group + 8] = moved.astype(BF).reshape(8, 2, 16, 128)

    seat = ((own["z0"] * 2 + own["y1"]) * 2 + own["y0"]) * 4 + own["x1"] * 2 + own["x0"]

    def message(chip):
        return pltpu.make_async_remote_copy(
            src_ref=mbuf.at[chip], dst_ref=lbuf.at[seat], send_sem=a2a.at[0], recv_sem=a2a.at[1],
            device_id=(role, 2 * chip + core), device_id_type=MESH,
        )

    def post(d, carry):
        message((dev // 2 + d) % CHIPS).start()
        return carry

    lax.fori_loop(1, CHIPS, post, 0)
    lbuf[seat] = mbuf[dev // 2]

    x1, x0 = own["x1"], own["x0"]
    lines = (
        (across("x1", "x0"), 1 - x1, 1 - x0), (across("x1"), 1 - x1, x0), (across("x0"), x1, 1 - x0),
    )

    arrivals = []
    for device, p1, p0 in lines:
        arrivals.append(sems.remote(resq.at[p1, p0], resx.at[x1, x0], resx.at[p1, p0], device))
        arrivals.append(sems.remote(wts, wx.at[x1, x0], wx.at[p1, p0], device))
    resx[x1, x0] = resq[x1, x0]
    wx[x1, x0] = wts[...]
    early = len(sems.pending)
    wg_wait = sems.remote(wg_hbm, wg.at[core], wg.at[sibling], twin)
    wu_wait = sems.remote(wu_hbm, wu.at[core], wu.at[sibling], twin)
    wd_waits = [
        sems.remote(wd_hbm.at[:, quarters[q]], wd.at[q, core], wd.at[q, sibling], twin) for q in range(4)
    ]

    late, sems.pending = sems.pending[early:], sems.pending[:early]

    spread = jnp.where(source == ((to % 64) // 4) * 16 + (to // 64) * 4 + to % 4, 1.0, 0.0).astype(BF)
    everyone = pltpu.make_async_remote_copy(
        src_ref=mbuf.at[pl.ds(0, CHIPS - 1)], dst_ref=lbuf.at[pl.ds(0, CHIPS - 1)],
        send_sem=a2a.at[0], recv_sem=a2a.at[1], device_id=twin, device_id_type=MESH,
    )
    everyone.wait_recv()
    for group in range(2):
        for head in range(2):
            rows = lbuf[16 * group:16 * group + 16, head].reshape(256, 128)
            moved = jnp.dot(spread, rows, preferred_element_type=F32).astype(BF)
            for c in range(4):
                rel[head, 64 * group:64 * group + 64, 128 * c:128 * c + 128] = moved[64 * c:64 * c + 64]

    def reduce_scatter(produce, buf, landing, dims, groups, pieces):
        found = all_pieces(groups, pieces)
        waits, before = [None] * len(found), len(sems.pending)

        def place(n, step, mine):
            _, columns, order, confined = found[n]
            indices = []
            for dim in dims:
                if dim in confined:
                    indices.append(confined[dim])
                    continue
                at = order.index(dim) if dim in order else len(order)
                here = own[dim] if mine else 1 - own[dim]
                indices.append(own[dim] if at < step else here if at == step else EVERY)
            return tuple(indices) + (EVERY, columns)

        def advance(n, step):
            order = found[n][2]
            mine, other = place(n, step, True), place(n, step, False)
            if step < len(order):
                waits[n] = sems.remote(buf.at[other], landing.at[mine], landing.at[other], across(order[step]))

        def add(n, step):
            waits[n]()
            mine, other = place(n, step, True), place(n, step, False)
            buf[mine] = buf[mine] + landing[other]

        for n, (_, columns, _, confined) in enumerate(found):
            if 1 not in confined.values():
                produce(buf, columns)
            advance(n, 0)
        sems.drain(before)
        rounds = len(groups[0][0])
        for step in range(1, rounds):
            for n in range(len(found)):
                add(n, step - 1)
                advance(n, step)
        result, last = [], []
        before = len(sems.pending)
        for at, (ring, direct) in enumerate(groups):
            columns = pl.ds(at * HALF, HALF)
            for n in range(len(found)):
                if found[n][0] == at:
                    add(n, rounds - 1)
            mine = tuple(own[dim] for dim in dims) + (EVERY, columns)
            others = []
            for flips in subsets(direct):
                other = tuple(1 - own[dim] if dim in flips else own[dim] for dim in dims) + (EVERY, columns)
                last.append(sems.remote(buf.at[other], landing.at[mine], landing.at[other], across(*flips)))
                others.append(other)
            result.append((columns, mine, others))
        sems.drain(before)
        for wait in last:
            wait()
        return result

    vw_load.wait()
    vw_wait()
    for head in range(2):
        values[:, HEAD * head:HEAD * head + HEAD] = jnp.dot(
            rel[head], vw[head], preferred_element_type=F32
        ).astype(BF)
    for copy in wo_loads:
        copy.wait()
    for wait in wo_waits:
        wait()

    def project(target, columns):
        width = columns.size
        weight = jnp.concatenate([wo[q, :, :, columns].reshape(2 * HEAD, width) for q in range(4)], axis=1)
        product = jnp.dot(values[...], weight, preferred_element_type=F32).astype(BF)
        for q in range(4):
            block = product[:, q * width:(q + 1) * width].reshape(2, 2, 2, 16, width)
            target[:, :, :, q // 2, q % 2, :, columns] = block

    summed = reduce_scatter(project, ab, rb, B_DIMS, B_GROUPS, B_PIECES)

    for wait in arrivals:
        wait()
    for j in range(4):
        hid[4 * j:4 * j + 4, :] = resx[j // 2, j % 2]
    block = tuple(own[dim] for dim in C_DIMS)
    squares = jnp.zeros((16, 1), F32)
    for columns, mine, others in summed:
        total = ab[mine].astype(F32)
        for other in others:
            total = total + rb[other].astype(F32)
        rounded = (hid[:, columns] + total).astype(BF)
        g[block + (EVERY, columns)] = rounded
        total = rounded.astype(F32)
        hid[:, columns] = total
        squares = squares + jnp.sum(total * total, axis=1, keepdims=True)

    direct_waits, before = [], len(sems.pending)
    for at, (_, direct) in enumerate(C_GROUPS):
        columns = pl.ds(at * HALF, HALF)
        here = g.at[block + (EVERY, columns)]
        waits = []
        for flips in subsets(direct):
            other = tuple(1 - own[dim] if dim in flips else own[dim] for dim in C_DIMS)
            waits.append(sems.remote(here, here, g.at[other + (EVERY, columns)], across(*flips)))
        direct_waits.append(waits)

    ss[0] = jnp.broadcast_to(squares, (16, 128))
    square_waits = [
        sems.remote(ss.at[0], ssr.at[x1, x0], ssr.at[p1, p0], device) for device, p1, p0 in lines
    ]
    sems.drain(before)
    for wait in square_waits:
        wait()
    squares = ss[0]
    for _, p1, p0 in lines:
        squares = squares + ssr[p1, p0]
    weights = jnp.concatenate([wx[j // 2, j % 2] for j in range(4)], axis=0)
    lanes = lax.broadcasted_iota(jnp.int32, (16, 128), 1)
    scale = lax.rsqrt(squares * (1.0 / D) + 1e-06)
    table_at = (own["z1"], own["z0"], own["y1"], own["y0"])
    tab[table_at] = jnp.where(lanes == EXPERTS, scale, weights)

    def table_step(first, second, others):
        dims = ("z1", "z0", "y1", "y0")

        def at(flips):
            indices = []
            for dim in dims:
                if dim in (first, second):
                    indices.append(1 - own[dim] if dim in flips else own[dim])
                else:
                    indices.append(EVERY if others else own[dim])
            return tuple(indices)

        return [
            sems.remote(tab.at[at(())], tab.at[at(())], tab.at[at(flips)], across(*flips))
            for flips in subsets((first, second))
        ]

    found = all_pieces(C_GROUPS, C_PIECES)
    waits = [None] * len(found)

    def gather_place(n, step, mine):
        _, columns, order, confined = found[n]
        indices = []
        for dim in C_DIMS:
            if dim in confined:
                indices.append(confined[dim])
            elif dim not in order or order.index(dim) < step:
                indices.append(EVERY)
            elif order.index(dim) == step:
                indices.append(own[dim] if mine else 1 - own[dim])
            else:
                indices.append(own[dim])
        return tuple(indices) + (EVERY, columns)

    table_waits = table_step("y0", "z0", False)
    for step in range(3):
        before = len(sems.pending)
        for n in range(len(found)):
            if step:
                waits[n]()
            elif n < 2:
                for wait in direct_waits[n]:
                    wait()
            here = g.at[gather_place(n, step, True)]
            there = g.at[gather_place(n, step, False)]
            waits[n] = sems.remote(here, here, there, across(found[n][2][step]))
        if step:
            sems.drain(before)
        if step < 2:
            for wait in table_waits:
                wait()
        if step == 0:
            table_waits = table_step("y1", "z1", True)

    wg_load.wait()
    wu_load.wait()
    wg_wait()
    wu_wait()
    for copy in wd_loads:
        copy.wait()
    for wait in wd_waits:
        wait()
    for copy in late:
        copy.wait_send()
    expert = role * 8 + zl * 4 + y
    rows_lanes = lax.broadcasted_iota(jnp.int32, (256, 128), 1)
    table = tab[...].reshape(256, 128)
    route = jnp.sum(jnp.where(rows_lanes == expert, table, 0.0), axis=1, keepdims=True)
    scale = jnp.sum(jnp.where(rows_lanes == EXPERTS, table, 0.0), axis=1, keepdims=True)
    batch, first = [], True
    for n, (_, columns, _, confined) in enumerate(found):
        waits[n]()
        if 0 not in confined.values():
            batch.append(columns)
        if n % 6 < 5 and n < len(found) - 1:
            continue
        rows = jnp.concatenate(
            [
                g[:, :, :, :, q // 2, q % 2, :, tile].reshape(256, tile.size)
                for tile in batch for q in range(4)
            ],
            axis=1,
        )
        for unit in range(2):
            for acc, weights in ((accg, wg), (accu, wu)):
                weight = jnp.concatenate(
                    [weights[unit, q, tile, :] for tile in batch for q in range(4)], axis=0
                )
                product = jnp.dot(rows, weight, preferred_element_type=F32)
                acc[unit] = product if first else acc[unit] + product
        batch, first = [], False
    for unit in range(2):
        gate = accg[unit] * scale
        activated = jax.nn.silu(gate) * (accu[unit] * scale) * route
        act[:, FF * unit:FF * unit + FF] = activated.astype(BF)

    def down(target, columns):
        width = columns.size
        weight = jnp.concatenate([wd[q, :, :, columns].reshape(2 * FF, width) for q in range(4)], axis=1)
        product = jnp.dot(act[...], weight, preferred_element_type=F32).astype(BF)
        for q in range(4):
            block = product[:, q * width:(q + 1) * width].reshape(2, 2, 2, 2, 16, width)
            target[:, :, :, :, q // 2, q % 2, :, columns] = block

    summed = reduce_scatter(down, ah, rh, C_DIMS, C_GROUPS, C_PIECES)
    for columns, mine, others in summed:
        total = hid[:, columns] + ah[mine].astype(F32)
        for other in others:
            total = total + rh[other].astype(F32)
        outs[:, columns] = total

    for j in range(4):
        fsend[j // 2, j % 2] = outs[4 * j:4 * j + 4, :]
    before = len(sems.pending)
    waits = [
        sems.remote(fsend.at[p1, p0], frecv.at[x1, x0], frecv.at[p1, p0], device)
        for device, p1, p0 in lines
    ]
    frecv[x1, x0] = fsend[x1, x0]
    everyone.wait_send()
    sems.drain(before)
    for wait in waits:
        wait()
    for j in range(4):
        out_ref[:, j * Q:(j + 1) * Q] = frecv[j // 2, j % 2].astype(BF)
    assert sems.count <= SEMS
    sems.drain(len(sems.pending))


def layer(*operands):
    vmem = pl.BlockSpec(memory_space=pltpu.VMEM)
    hbm = pl.BlockSpec(memory_space=pl.ANY)
    b_shape, c_shape = (2,) * 5 + (16, Q), (2,) * 6 + (16, Q)
    return pl.pallas_call(
        kernel,
        out_shape=jax.ShapeDtypeStruct((4, D), BF),
        in_specs=[pl.BlockSpec(memory_space=pltpu.SMEM)] + [vmem] * 3 + [hbm] * 7,
        out_specs=vmem,
        scratch_shapes=[
            pltpu.VMEM((4, HEADS, LATENT), BF),
            pltpu.VMEM((4, LATENT, LEN), BF),
            pltpu.VMEM((4, HEADS, KEY_VALUE_RANK), BF),
            pltpu.VMEM((CHIPS, 2, 16, 128), BF),
            pltpu.VMEM((CHIPS, 2, 16, 128), BF),
            pltpu.VMEM((2, 128, KEY_VALUE_RANK), BF),
            pltpu.VMEM((2, 2, 4, Q), F32),
            pltpu.VMEM((4, 128), F32),
            pltpu.SemaphoreType.DMA((2,)),
            pltpu.VMEM((2, KEY_VALUE_RANK, HEAD), BF),
            pltpu.VMEM((4, 2, HEAD, Q), BF),
            pltpu.VMEM((2, 4, Q, FF), BF),
            pltpu.VMEM((2, 4, Q, FF), BF),
            pltpu.VMEM((4, 2, FF, Q), BF),
            pltpu.VMEM((2, 2, 4, Q), F32),
            pltpu.VMEM((2, 2, 4, 128), F32),
            pltpu.VMEM((16, Q), F32),
            pltpu.VMEM((128, 2 * HEAD), BF),
            pltpu.VMEM(b_shape, BF),
            pltpu.VMEM(b_shape, BF),
            pltpu.VMEM((1, 16, 128), F32),
            pltpu.VMEM((2, 2, 16, 128), F32),
            pltpu.VMEM((2,) * 4 + (16, 128), F32),
            pltpu.VMEM(c_shape, BF),
            pltpu.VMEM((2, 256, FF), F32),
            pltpu.VMEM((2, 256, FF), F32),
            pltpu.VMEM((256, 2 * FF), BF),
            pltpu.VMEM(c_shape, BF),
            pltpu.VMEM(c_shape, BF),
            pltpu.VMEM((16, Q), F32),
            pltpu.VMEM((2, 2, 4, Q), F32),
            pltpu.VMEM((2, 2, 4, Q), F32),
            pltpu.SemaphoreType.DMA((19,)),
            pltpu.SemaphoreType.DMA((SEMS,)),
            pltpu.SemaphoreType.DMA((SEMS,)),
        ],
        compiler_params=pltpu.CompilerParams(
            collective_id=0, has_side_effects=True, vmem_limit_bytes=58 * 2**20
        ),
    )(*operands)


def local(
    queries, latent_cache, cache_lengths, residual, expert_ids, route_weights,
    value_weight, w_out, w_gate, w_up, w_down,
):
    return layer(
        cache_lengths, residual, expert_ids, route_weights, value_weight[0], queries, latent_cache.transpose(0, 2, 1), w_out,
        w_gate.reshape(4, Q, FF), w_up.reshape(4, Q, FF), w_down[0],
    )


def solution(mesh):
    return jax.shard_map(
        local,
        mesh=mesh,
        in_specs=(
            P(("role", "dev"), None, None),
            P(("role", "dev"), None, None),
            P(("role", "dev")),
            P(("role", "dev"), None),
            P(("role", "dev"), None),
            P(("role", "dev"), None),
            P("dev", None, None),
            P("dev", None),
            P(("role", "dev"), None, None),
            P(("role", "dev"), None, None),
            P(("role", "dev"), None, None),
        ),
        out_specs=P(("role", "dev"), None),
        check_vma=False,
    )
```

```python
import math

import jax
import jax.numpy as jnp
from jax import lax
from jax.experimental import pallas as pl
from jax.experimental.pallas import tpu as pltpu
from jax.sharding import PartitionSpec as P

KEY_VALUE_RANK = 512
HEADS = 64
CHIPS = HEADS // 2
LEN = 512
LATENT = 576
EXPERTS = 16
MESH = pl.DeviceIdType.MESH
D = 7168
Q = D // 4
FF = 256
HEAD = 128
BF = jnp.bfloat16
F32 = jnp.float32
score_scale = 1.0 / math.sqrt(192.0)


B_DIMS = ("z0", "y1", "y0", "x1", "x0")
C_DIMS = ("z1",) + B_DIMS
HALF = Q // 2
B_GROUPS = ((("x1", "y1"), ("x0", "y0", "z0")), (("x0", "y0"), ("x1", "y1", "z0")))
B_PIECES = (
    (0, 2, 0, None), (3, 2, 1, None), (2, 1, 0, None), (5, 1, 1, None), (6, 1, 0, 0), (6, 1, 1, 1),
)
C_GROUPS = ((("x1", "y1", "z1"), ("x0", "y0", "z0")), (("x0", "y0", "z0"), ("x1", "y1", "z1")))
C_PIECES = (
    (0, 1, 0, None), (3, 1, 1, None), (5, 1, 2, None), (1, 1, 0, None), (4, 1, 1, None), (6, 1, 2, None),
    (2, 1, 0, 0), (2, 1, 1, 1),
)


def all_pieces(groups, pieces):
    found = []
    for tile, count, turn, half in pieces:
        for at, (ring, direct) in enumerate(groups):
            columns = pl.ds(at * HALF + tile * 128, count * 128)
            found.append((at, columns, ring[turn:] + ring[:turn], {} if half is None else {direct[0]: half}))
    return found


def subsets(bits):
    found = [tuple(bit for i, bit in enumerate(bits) if n >> i & 1) for n in range(1, 2 ** len(bits))]
    return sorted(found, key=lambda flips: -len(flips))


EVERY = slice(None)


class Sems:
    def __init__(self, sends, recvs):
        self.sends, self.recvs, self.count, self.pending = sends, recvs, 0, []

    def drain(self, count):
        for copy in self.pending[:count]:
            copy.wait_send()
        self.pending = self.pending[count:]

    def remote(self, source, target, landing, device):
        n = self.count
        self.count += 1
        copy = pltpu.make_async_remote_copy(
            src_ref=source,
            dst_ref=target,
            send_sem=self.sends.at[n],
            recv_sem=self.recvs.at[n],
            device_id=device,
            device_id_type=MESH,
        )
        copy.start()
        self.pending.append(copy)
        return pltpu.make_async_remote_copy(
            src_ref=source,
            dst_ref=landing,
            send_sem=self.sends.at[n],
            recv_sem=self.recvs.at[n],
            device_id=device,
            device_id_type=MESH,
        ).wait_recv


SEMS = 196


def kernel(
    len_ref, res_ref, ids_ref, rw_ref, vw_hbm, q_hbm, cache_hbm, wo_hbm, wg_hbm, wu_hbm, wd_hbm, out_ref,
    qv, cv, lat, mbuf, lbuf, rel, resq, wts, a2a, vw, wo, wg, wu, wd, resx, wx, hid, values, ab, rb, ss, ssr, tab, g,
    accg, accu, act, ah, rh, outs, fsend, frecv, loads, sends, recvs,
):
    role, dev = lax.axis_index("role"), lax.axis_index("dev")
    core, x, y, zl = dev % 2, (dev // 2) % 4, (dev // 8) % 4, dev // 32
    own = {
        "x1": x // 2, "x0": (x + x // 2) % 2, "y1": y // 2, "y0": (y + y // 2) % 2,
        "z1": role, "z0": (zl + role) % 2,
    }
    def across(*flips):
        at = {bit: 1 - own[bit] if bit in flips else own[bit] for bit in own}
        to_x = 2 * at["x1"] + (at["x1"] + at["x0"]) % 2
        to_y = 2 * at["y1"] + (at["y1"] + at["y0"]) % 2
        to_zl = (at["z1"] + at["z0"]) % 2
        return at["z1"], ((to_zl * 4 + to_y) * 4 + to_x) * 2 + core

    twin = (role, dev + 1 - 2 * core)
    sibling = 1 - core

    fetch = []

    def load(source, target):
        copy = pltpu.make_async_copy(source, target, loads.at[len(fetch)])
        copy.start()
        fetch.append(copy)
        return copy

    attention_loads = [(load(q_hbm.at[n], qv.at[n]), load(cache_hbm.at[n], cv.at[n])) for n in range(4)]
    vw_load = load(vw_hbm, vw.at[core])
    quarters = [pl.ds(q * Q, Q) for q in range(4)]
    wo_loads = [load(wo_hbm.at[:, quarters[q]], wo.at[q, core]) for q in range(4)]
    wg_load, wu_load = load(wg_hbm, wg.at[core]), load(wu_hbm, wu.at[core])
    wd_loads = [load(wd_hbm.at[:, quarters[q]], wd.at[q, core]) for q in range(4)]

    sems = Sems(sends, recvs)
    barrier = pltpu.get_barrier_semaphore()

    def greet(d, carry):
        pl.semaphore_signal(barrier, inc=1, device_id=(role, (dev + 2 * d) % HEADS), device_id_type=MESH)
        return carry

    lax.fori_loop(1, CHIPS, greet, 0)
    beyond = [across(*flips) for flips in subsets(("x1", "y1", "z1")) if "z1" in flips]
    for device in [twin] + beyond:
        pl.semaphore_signal(barrier, inc=1, device_id=device, device_id_type=MESH)

    for q in range(4):
        resq[q // 2, q % 2] = res_ref[:, q * Q:(q + 1) * Q].astype(F32)
    four_lanes = lax.broadcasted_iota(jnp.int32, (4, 128), 1)
    dense = jnp.zeros((4, 128), F32)
    for k in range(8):
        dense = dense + jnp.where(four_lanes == ids_ref[:, k:k + 1], rw_ref[:, k:k + 1], 0.0)
    wts[...] = dense

    slots = lax.broadcasted_iota(jnp.int32, (HEADS, LEN), 1)
    for pair in attention_loads:
        for copy in pair:
            copy.wait()
    def attend(requests):
        scores = [jnp.dot(qv[n], cv[n], preferred_element_type=F32) * score_scale for n in requests]
        for n, score in zip(requests, scores):
            live = jnp.where(slots < len_ref[n], score, -jnp.inf)
            raised = jnp.exp(live - jnp.max(live, axis=1, keepdims=True))
            chances = (raised / jnp.sum(raised, axis=1, keepdims=True)).astype(BF)
            lat[n] = lax.dot_general(
                chances, cv[n, :KEY_VALUE_RANK, :], (((1,), (1,)), ((), ())), preferred_element_type=F32
            ).astype(BF)

    attend((0, 1, 2, 3))

    to = lax.broadcasted_iota(jnp.int32, (256, 256), 0)
    source = lax.broadcasted_iota(jnp.int32, (256, 256), 1)
    regroup = jnp.where(source == (to % 16) * 16 + to // 16, 1.0, 0.0).astype(BF)
    for group in range(4):
        heads = slice(16 * group, 16 * group + 16)
        pieces = [lat[n, heads, 128 * c:128 * c + 128] for c in range(4) for n in range(4)]
        moved = jnp.dot(regroup, jnp.concatenate(pieces, axis=0), preferred_element_type=F32)
        mbuf[8 * group:8 * group + 8] = moved.astype(BF).reshape(8, 2, 16, 128)

    pl.semaphore_wait(barrier, CHIPS + len(beyond))
    seat = ((own["z0"] * 2 + own["y1"]) * 2 + own["y0"]) * 4 + own["x1"] * 2 + own["x0"]

    def message(chip):
        return pltpu.make_async_remote_copy(
            src_ref=mbuf.at[chip], dst_ref=lbuf.at[seat], send_sem=a2a.at[0], recv_sem=a2a.at[1],
            device_id=(role, 2 * chip + core), device_id_type=MESH,
        )

    def post(d, carry):
        message((dev // 2 + d) % CHIPS).start()
        return carry

    lax.fori_loop(1, CHIPS, post, 0)
    lbuf[seat] = mbuf[dev // 2]

    x1, x0 = own["x1"], own["x0"]
    lines = (
        (across("x1", "x0"), 1 - x1, 1 - x0), (across("x1"), 1 - x1, x0), (across("x0"), x1, 1 - x0),
    )

    vw_wait = sems.remote(vw_hbm, vw.at[core], vw.at[sibling], twin)
    wo_waits = [
        sems.remote(wo_hbm.at[:, quarters[q]], wo.at[q, core], wo.at[q, sibling], twin) for q in range(4)
    ]

    arrivals = []
    for device, p1, p0 in lines:
        arrivals.append(sems.remote(resq.at[p1, p0], resx.at[x1, x0], resx.at[p1, p0], device))
        arrivals.append(sems.remote(wts, wx.at[x1, x0], wx.at[p1, p0], device))
    resx[x1, x0] = resq[x1, x0]
    wx[x1, x0] = wts[...]
    early = len(sems.pending)
    wg_wait = sems.remote(wg_hbm, wg.at[core], wg.at[sibling], twin)
    wu_wait = sems.remote(wu_hbm, wu.at[core], wu.at[sibling], twin)
    wd_waits = [
        sems.remote(wd_hbm.at[:, quarters[q]], wd.at[q, core], wd.at[q, sibling], twin) for q in range(4)
    ]

    late, sems.pending = sems.pending[early:], sems.pending[:early]

    spread = jnp.where(source == ((to % 64) // 4) * 16 + (to // 64) * 4 + to % 4, 1.0, 0.0).astype(BF)
    everyone = pltpu.make_async_remote_copy(
        src_ref=mbuf.at[pl.ds(0, CHIPS - 1)], dst_ref=lbuf.at[pl.ds(0, CHIPS - 1)],
        send_sem=a2a.at[0], recv_sem=a2a.at[1], device_id=twin, device_id_type=MESH,
    )
    everyone.wait_recv()
    for group in range(2):
        for head in range(2):
            rows = lbuf[16 * group:16 * group + 16, head].reshape(256, 128)
            moved = jnp.dot(spread, rows, preferred_element_type=F32).astype(BF)
            for c in range(4):
                rel[head, 64 * group:64 * group + 64, 128 * c:128 * c + 128] = moved[64 * c:64 * c + 64]

    def reduce_scatter(produce, buf, landing, dims, groups, pieces):
        found = all_pieces(groups, pieces)
        waits, before = [None] * len(found), len(sems.pending)

        def place(n, step, mine):
            _, columns, order, confined = found[n]
            indices = []
            for dim in dims:
                if dim in confined:
                    indices.append(confined[dim])
                    continue
                at = order.index(dim) if dim in order else len(order)
                here = own[dim] if mine else 1 - own[dim]
                indices.append(own[dim] if at < step else here if at == step else EVERY)
            return tuple(indices) + (EVERY, columns)

        def advance(n, step):
            order = found[n][2]
            mine, other = place(n, step, True), place(n, step, False)
            if step < len(order):
                waits[n] = sems.remote(buf.at[other], landing.at[mine], landing.at[other], across(order[step]))

        def add(n, step):
            waits[n]()
            mine, other = place(n, step, True), place(n, step, False)
            buf[mine] = buf[mine] + landing[other]

        for n, (_, columns, _, confined) in enumerate(found):
            if 1 not in confined.values():
                produce(buf, columns)
            advance(n, 0)
        sems.drain(before)
        rounds = len(groups[0][0])
        for step in range(1, rounds):
            for n in range(len(found)):
                add(n, step - 1)
                advance(n, step)
        result = []
        before = len(sems.pending)
        for at, (ring, direct) in enumerate(groups):
            columns = pl.ds(at * HALF, HALF)
            for n in range(len(found)):
                if found[n][0] == at:
                    add(n, rounds - 1)
            mine = tuple(own[dim] for dim in dims) + (EVERY, columns)
            others, last = [], []
            for flips in subsets(direct):
                other = tuple(1 - own[dim] if dim in flips else own[dim] for dim in dims) + (EVERY, columns)
                last.append(sems.remote(buf.at[other], landing.at[mine], landing.at[other], across(*flips)))
                others.append(other)
            result.append((columns, mine, others, last))
        sems.drain(before)
        return result

    vw_load.wait()
    vw_wait()
    for head in range(2):
        values[:, HEAD * head:HEAD * head + HEAD] = jnp.dot(
            rel[head], vw[head], preferred_element_type=F32
        ).astype(BF)
    for copy in wo_loads:
        copy.wait()
    for wait in wo_waits:
        wait()

    def project(target, columns):
        width = columns.size
        weight = jnp.concatenate([wo[q, :, :, columns].reshape(2 * HEAD, width) for q in range(4)], axis=1)
        product = jnp.dot(values[...], weight, preferred_element_type=F32).astype(BF)
        for q in range(4):
            block = product[:, q * width:(q + 1) * width].reshape(2, 2, 2, 16, width)
            target[:, :, :, q // 2, q % 2, :, columns] = block

    summed = reduce_scatter(project, ab, rb, B_DIMS, B_GROUPS, B_PIECES)

    for wait in arrivals:
        wait()
    for j in range(4):
        hid[4 * j:4 * j + 4, :] = resx[j // 2, j % 2]
    block = tuple(own[dim] for dim in C_DIMS)
    squares = jnp.zeros((16, 1), F32)
    direct_waits, before = [], len(sems.pending)
    for (columns, mine, others, last), (_, direct) in zip(summed, C_GROUPS):
        for wait in last:
            wait()
        total = ab[mine].astype(F32)
        for other in others:
            total = total + rb[other].astype(F32)
        rounded = (hid[:, columns] + total).astype(BF)
        g[block + (EVERY, columns)] = rounded
        here = g.at[block + (EVERY, columns)]
        waits = []
        for flips in subsets(direct):
            other = tuple(1 - own[dim] if dim in flips else own[dim] for dim in C_DIMS)
            waits.append(sems.remote(here, here, g.at[other + (EVERY, columns)], across(*flips)))
        direct_waits.append(waits)
        total = rounded.astype(F32)
        hid[:, columns] = total
        squares = squares + jnp.sum(total * total, axis=1, keepdims=True)

    ss[0] = jnp.broadcast_to(squares, (16, 128))
    square_waits = [
        sems.remote(ss.at[0], ssr.at[x1, x0], ssr.at[p1, p0], device) for device, p1, p0 in lines
    ]
    sems.drain(before)
    for wait in square_waits:
        wait()
    squares = ss[0]
    for _, p1, p0 in lines:
        squares = squares + ssr[p1, p0]
    weights = jnp.concatenate([wx[j // 2, j % 2] for j in range(4)], axis=0)
    lanes = lax.broadcasted_iota(jnp.int32, (16, 128), 1)
    scale = lax.rsqrt(squares * (1.0 / D) + 1e-06)
    table_at = (own["z1"], own["z0"], own["y1"], own["y0"])
    tab[table_at] = jnp.where(lanes == EXPERTS, scale, weights)

    def table_step(first, second, others):
        dims = ("z1", "z0", "y1", "y0")

        def at(flips):
            indices = []
            for dim in dims:
                if dim in (first, second):
                    indices.append(1 - own[dim] if dim in flips else own[dim])
                else:
                    indices.append(EVERY if others else own[dim])
            return tuple(indices)

        return [
            sems.remote(tab.at[at(())], tab.at[at(())], tab.at[at(flips)], across(*flips))
            for flips in subsets((first, second))
        ]

    found = all_pieces(C_GROUPS, C_PIECES)
    waits = [None] * len(found)

    def gather_place(n, step, mine):
        _, columns, order, confined = found[n]
        indices = []
        for dim in C_DIMS:
            if dim in confined:
                indices.append(confined[dim])
            elif dim not in order or order.index(dim) < step:
                indices.append(EVERY)
            elif order.index(dim) == step:
                indices.append(own[dim] if mine else 1 - own[dim])
            else:
                indices.append(own[dim])
        return tuple(indices) + (EVERY, columns)

    table_waits = table_step("y0", "z0", False)
    for step in range(3):
        before = len(sems.pending)
        for n in range(len(found)):
            if step:
                waits[n]()
            elif n < 2:
                for wait in direct_waits[n]:
                    wait()
            here = g.at[gather_place(n, step, True)]
            there = g.at[gather_place(n, step, False)]
            waits[n] = sems.remote(here, here, there, across(found[n][2][step]))
        if step:
            sems.drain(before)
        if step < 2:
            for wait in table_waits:
                wait()
        if step == 0:
            table_waits = table_step("y1", "z1", True)

    wg_load.wait()
    wu_load.wait()
    wg_wait()
    wu_wait()
    for copy in wd_loads:
        copy.wait()
    for wait in wd_waits:
        wait()
    for copy in late:
        copy.wait_send()
    expert = role * 8 + zl * 4 + y
    rows_lanes = lax.broadcasted_iota(jnp.int32, (256, 128), 1)
    table = tab[...].reshape(256, 128)
    route = jnp.sum(jnp.where(rows_lanes == expert, table, 0.0), axis=1, keepdims=True)
    scale = jnp.sum(jnp.where(rows_lanes == EXPERTS, table, 0.0), axis=1, keepdims=True)
    batch, first = [], True
    for n, (_, columns, _, confined) in enumerate(found):
        waits[n]()
        if 0 not in confined.values():
            batch.append(columns)
        if n % 6 < 5 and n < len(found) - 1:
            continue
        rows = jnp.concatenate(
            [
                g[:, :, :, :, q // 2, q % 2, :, tile].reshape(256, tile.size)
                for tile in batch for q in range(4)
            ],
            axis=1,
        )
        for unit in range(2):
            for acc, weights in ((accg, wg), (accu, wu)):
                weight = jnp.concatenate(
                    [weights[unit, q, tile, :] for tile in batch for q in range(4)], axis=0
                )
                product = jnp.dot(rows, weight, preferred_element_type=F32)
                acc[unit] = product if first else acc[unit] + product
        batch, first = [], False
    for unit in range(2):
        gate = accg[unit] * scale
        activated = jax.nn.silu(gate) * (accu[unit] * scale) * route
        act[:, FF * unit:FF * unit + FF] = activated.astype(BF)

    def down(target, columns):
        width = columns.size
        weight = jnp.concatenate([wd[q, :, :, columns].reshape(2 * FF, width) for q in range(4)], axis=1)
        product = jnp.dot(act[...], weight, preferred_element_type=F32).astype(BF)
        for q in range(4):
            block = product[:, q * width:(q + 1) * width].reshape(2, 2, 2, 2, 16, width)
            target[:, :, :, :, q // 2, q % 2, :, columns] = block

    summed = reduce_scatter(down, ah, rh, C_DIMS, C_GROUPS, C_PIECES)
    before, waits = len(sems.pending), []
    for columns, mine, others, last in summed:
        for wait in last:
            wait()
        total = hid[:, columns] + ah[mine].astype(F32)
        for other in others:
            total = total + rh[other].astype(F32)
        outs[:, columns] = total
        for j in range(4):
            fsend[j // 2, j % 2, :, columns] = outs[4 * j:4 * j + 4, columns]
        for device, p1, p0 in lines:
            tail = (EVERY, columns)
            waits.append(
                sems.remote(fsend.at[(p1, p0) + tail], frecv.at[(x1, x0) + tail], frecv.at[(p1, p0) + tail], device)
            )
    frecv[x1, x0] = fsend[x1, x0]
    everyone.wait_send()
    sems.drain(before)
    for wait in waits:
        wait()
    for j in range(4):
        out_ref[:, j * Q:(j + 1) * Q] = frecv[j // 2, j % 2].astype(BF)
    assert sems.count <= SEMS
    sems.drain(len(sems.pending))


def layer(*operands):
    vmem = pl.BlockSpec(memory_space=pltpu.VMEM)
    hbm = pl.BlockSpec(memory_space=pl.ANY)
    b_shape, c_shape = (2,) * 5 + (16, Q), (2,) * 6 + (16, Q)
    return pl.pallas_call(
        kernel,
        out_shape=jax.ShapeDtypeStruct((4, D), BF),
        in_specs=[pl.BlockSpec(memory_space=pltpu.SMEM)] + [vmem] * 3 + [hbm] * 7,
        out_specs=vmem,
        scratch_shapes=[
            pltpu.VMEM((4, HEADS, LATENT), BF),
            pltpu.VMEM((4, LATENT, LEN), BF),
            pltpu.VMEM((4, HEADS, KEY_VALUE_RANK), BF),
            pltpu.VMEM((CHIPS, 2, 16, 128), BF),
            pltpu.VMEM((CHIPS, 2, 16, 128), BF),
            pltpu.VMEM((2, 128, KEY_VALUE_RANK), BF),
            pltpu.VMEM((2, 2, 4, Q), F32),
            pltpu.VMEM((4, 128), F32),
            pltpu.SemaphoreType.DMA((2,)),
            pltpu.VMEM((2, KEY_VALUE_RANK, HEAD), BF),
            pltpu.VMEM((4, 2, HEAD, Q), BF),
            pltpu.VMEM((2, 4, Q, FF), BF),
            pltpu.VMEM((2, 4, Q, FF), BF),
            pltpu.VMEM((4, 2, FF, Q), BF),
            pltpu.VMEM((2, 2, 4, Q), F32),
            pltpu.VMEM((2, 2, 4, 128), F32),
            pltpu.VMEM((16, Q), F32),
            pltpu.VMEM((128, 2 * HEAD), BF),
            pltpu.VMEM(b_shape, BF),
            pltpu.VMEM(b_shape, BF),
            pltpu.VMEM((1, 16, 128), F32),
            pltpu.VMEM((2, 2, 16, 128), F32),
            pltpu.VMEM((2,) * 4 + (16, 128), F32),
            pltpu.VMEM(c_shape, BF),
            pltpu.VMEM((2, 256, FF), F32),
            pltpu.VMEM((2, 256, FF), F32),
            pltpu.VMEM((256, 2 * FF), BF),
            pltpu.VMEM(c_shape, BF),
            pltpu.VMEM(c_shape, BF),
            pltpu.VMEM((16, Q), F32),
            pltpu.VMEM((2, 2, 4, Q), F32),
            pltpu.VMEM((2, 2, 4, Q), F32),
            pltpu.SemaphoreType.DMA((19,)),
            pltpu.SemaphoreType.DMA((SEMS,)),
            pltpu.SemaphoreType.DMA((SEMS,)),
        ],
        compiler_params=pltpu.CompilerParams(
            collective_id=0, has_side_effects=True, vmem_limit_bytes=58 * 2**20
        ),
    )(*operands)


def local(
    queries, latent_cache, cache_lengths, residual, expert_ids, route_weights,
    value_weight, w_out, w_gate, w_up, w_down,
):
    return layer(
        cache_lengths, residual, expert_ids, route_weights, value_weight[0], queries, latent_cache.transpose(0, 2, 1), w_out,
        w_gate.reshape(4, Q, FF), w_up.reshape(4, Q, FF), w_down[0],
    )


def solution(mesh):
    return jax.shard_map(
        local,
        mesh=mesh,
        in_specs=(
            P(("role", "dev"), None, None),
            P(("role", "dev"), None, None),
            P(("role", "dev")),
            P(("role", "dev"), None),
            P(("role", "dev"), None),
            P(("role", "dev"), None),
            P("dev", None, None),
            P("dev", None),
            P(("role", "dev"), None, None),
            P(("role", "dev"), None, None),
            P(("role", "dev"), None, None),
        ),
        out_specs=P(("role", "dev"), None),
        check_vma=False,
    )
```
